32 devices in a mesh: tm: 4 (over x, core), ctx: 8 (over z, y).
Axes of the slice: x: 2, y: 2, z: 4, core: 2. Of those that a mesh axis runs over, the one named last changes fastest.
Arguments:
- iterate: float32 [4, 1344, 1536], P('tm', 'ctx'), may hold values from -6 to 6
- anchor: float32 [1344, 1536], P('ctx'), may hold values from -6 to 6
- frame_index: int32 [1344], P('ctx'), may hold values from 0 to 7, never falling along the last dimension, each value on 1 to 336 neighbouring positions
- noise_steps: int32 [4, 8], P('tm'), may hold values from 0 to 11
- qkv_weight: bfloat16 [1536, 4608], replicated, may hold values from -0.15625 to 0.15625
- out_weight: bfloat16 [1536, 1536], replicated, may hold values from -0.15625 to 0.15625
- mod_weight: bfloat16 [256, 4608], replicated, may hold values from -0.375 to 0.375
Outputs:
- updated: float32 [4, 1344, 1536], P('tm', 'ctx')
The draws below stay inside these ranges and needn't reach their ends.
Inputs may be any that keep to these rules, and one draw needn't show every extreme that they name: `frame_index`: frame numbers never fall along the sequence; each of the 8 frames holds 1 to 336 tokens.
All inputs are finite; a program needn't handle non-finite values.
Results may differ from the reference program's by a relative error of at most 0.00051.
Values may be sent and summed in bfloat16 or wider, within the bound.
A program may use at most 192 MiB of HBM per device.

```python
import math
import jax
import jax.numpy as jnp
import numpy as np
from jax import lax

D = 1536
HEADS = 12
HD = 128
FREQ = 256
NSCHED = 12
L = 1344
TSTEPS = 4
NF = 8
FMAX = 336


def with_ends(result, stream_key, smallest, high):
    extent = result.shape
    place = [jax.random.randint(jax.random.fold_in(stream_key, axis), (), 0, extent[axis]) for axis in range(len(extent))]
    result = result.at[tuple(place)].set(smallest)
    longest = extent.index(max(extent))
    place[longest] = (place[longest] + 1) % extent[longest]
    return result.at[tuple(place)].set(high)


def level_of(own_key, dims, shards, smallest, high):
    level, own = 1.0, jax.random.fold_in(own_key, 6)
    for position, parts in shards:
        heights = jnp.exp(jax.random.uniform(jax.random.fold_in(own, position), (parts,), jnp.float32, smallest / len(shards), high / len(shards)))
        level = level * jnp.repeat(heights, dims[position] // parts).reshape([-1 if axis == position else 1 for axis in range(len(dims))])
    return level


def length_profile(count, total, reach, slope):
    weights = [(1 << 20) // math.isqrt(rank ** slope) + 1 for rank in range(2, count + 1)]
    spare, holding = total - reach - (count - 1), [1] * (count - 1)
    while spare > 0:
        candidates = [i for i in range(count - 1) if holding[i] < reach]
        pool, budget = sum([weights[i] for i in candidates]), spare
        for i in candidates:
            extra = min(reach - holding[i], max(1, budget * weights[i] // pool), spare)
            holding[i] = holding[i] + extra
            spare = spare - extra
    return np.array([reach] + holding)


def uneven(own_key, count, total, bound, skew):
    if count == 2:
        one = jax.random.randint(own_key, (), max(1, total - bound), min(bound, total - 1) + 1)
        return jnp.stack([one, total - one])
    lengths = jnp.asarray(length_profile(count, total, bound, skew), jnp.int32)
    couples = (count - 1) // 2
    donor, taker = lengths[1:1 + 2 * couples:2], lengths[2:2 + 2 * couples:2]
    slack = jnp.minimum(donor - 1, bound - taker)
    passed = jax.random.randint(jax.random.fold_in(own_key, 1), (couples,), 0, 1 << 20) % (slack + 1)
    lengths = lengths.at[1:1 + 2 * couples:2].set(donor - passed).at[2:2 + 2 * couples:2].set(taker + passed)
    return lengths[jax.random.permutation(jax.random.fold_in(own_key, 2), count)]


def noise(key, shape, scale, limit, cuts=(), kind=jnp.bfloat16):
    drawn = jax.random.normal(key, shape, jnp.float32) * scale
    if len(cuts) > 0:
        drawn = level_of(key, shape, cuts, -0.22, 0.18) * drawn
    return jnp.clip(drawn, min=-limit, max=limit).astype(kind)


def setup_inputs(seed: int = 0) -> dict:
    arg_keys = jax.random.split(jax.random.key(seed), 8)
    return {
        "iterate": noise(arg_keys[0], (TSTEPS, L, D), 1.0, 6.0, ((0, 4), (1, 8)), jnp.float32),
        "anchor": noise(arg_keys[1], (L, D), 1.0, 6.0, ((0, 8),), jnp.float32),
        "frame_index": jnp.searchsorted(jnp.cumsum(uneven(arg_keys[2], NF, L, FMAX, 0)), jnp.arange(L), side="right").astype(jnp.int32),
        "noise_steps": with_ends(jax.random.randint(arg_keys[3], (TSTEPS, NF), 0, NSCHED), jax.random.fold_in(arg_keys[3], 1), 0, NSCHED - 1).astype(jnp.int32),
        "qkv_weight": noise(arg_keys[4], (D, 3 * D), D ** -0.5, 0.15625),
        "out_weight": noise(arg_keys[5], (D, D), D ** -0.5, 0.15625),
        "mod_weight": noise(arg_keys[6], (FREQ, 3 * D), FREQ ** -0.5, 0.375),
    }


shift_factor = 5.0
norm_eps = 1e-06

def noise_level(level_index):
    fraction = level_index / NSCHED
    return shift_factor * fraction / (1.0 + (shift_factor - 1.0) * fraction)

def frame_terms(steps_row, mod_weight):
    level_float = steps_row.astype(jnp.float32)
    upper = noise_level(level_float + 1.0)
    lower = noise_level(level_float)
    step_size = upper - lower
    half_freq = FREQ // 2
    rates = jnp.exp(-math.log(10000.0) * jnp.arange(half_freq, dtype=jnp.float32) / half_freq)
    angles = (1000.0 * upper)[:, None] * rates[None, :]
    features = jnp.concatenate([jnp.cos(angles), jnp.sin(angles)], axis=1).astype(jnp.bfloat16)
    modulation = jnp.dot(features, mod_weight, preferred_element_type=jnp.float32)
    return (modulation, step_size)

def layer_norm(latent):
    center = latent - lax.optimization_barrier(jnp.mean(latent, axis=-1, keepdims=True))
    spread = lax.optimization_barrier(jnp.mean(center * center, axis=-1, keepdims=True))
    return center * lax.rsqrt(spread + norm_eps)

def head_norm(projected):
    tok_rows = projected.shape[0]
    split = projected.reshape(tok_rows, HEADS, HD)
    scaled = split * lax.rsqrt(lax.optimization_barrier(jnp.mean(split * split, axis=-1, keepdims=True)) + norm_eps)
    return scaled.reshape(tok_rows, D).astype(jnp.bfloat16)

def velocity_drift(latent, steps_row, frame_index, qkv_weight, out_weight, mod_weight):
    modulation, step_size = frame_terms(steps_row, mod_weight)
    tok_mod = modulation[frame_index]
    tok_step = step_size[frame_index]
    shift_part = tok_mod[:, :D]
    scale_part = tok_mod[:, D:2 * D]
    gate_part = tok_mod[:, 2 * D:]
    normed = (layer_norm(latent) * (1.0 + scale_part) + shift_part).astype(jnp.bfloat16)
    projected = jnp.dot(normed, qkv_weight, preferred_element_type=jnp.float32)
    queries = head_norm(projected[:, :D])
    key_rows = head_norm(projected[:, D:2 * D])
    values = projected[:, 2 * D:].astype(jnp.bfloat16)
    query_heads = queries.reshape(L, HEADS, HD).transpose(1, 0, 2)
    key_heads = key_rows.reshape(L, HEADS, HD).transpose(1, 0, 2)
    value_heads = values.reshape(L, HEADS, HD).transpose(1, 0, 2)
    allowed = frame_index[None, :] <= frame_index[:, None]

    def one_head(operands):
        query_one, key_one, value_one = operands
        scores = jnp.dot(query_one, key_one.T, preferred_element_type=jnp.float32) * HD ** (-0.5)
        weights = jnp.where(allowed, jnp.exp(scores), 0.0)
        denominator = lax.optimization_barrier(jnp.sum(weights, axis=-1))
        numerator = jnp.dot(weights.astype(jnp.bfloat16), value_one, preferred_element_type=jnp.float32)
        return (numerator / denominator[:, None]).astype(jnp.bfloat16)
    head_outputs = lax.map(one_head, (query_heads, key_heads, value_heads))
    attended = head_outputs.transpose(1, 0, 2).reshape(L, D)
    branch = jnp.dot(attended, out_weight, preferred_element_type=jnp.float32)
    return -tok_step[:, None] * (latent + gate_part * branch)

def reference(iterate, anchor, frame_index, noise_steps, qkv_weight, out_weight, mod_weight):

    def advance(running, operands):
        latent, steps_row = operands
        running = running + velocity_drift(latent, steps_row, frame_index, qkv_weight, out_weight, mod_weight)
        return (running, running)
    _, partial_sums = lax.scan(advance, jnp.zeros((L, D), jnp.float32), (iterate, noise_steps))
    return anchor[None, :, :] + partial_sums
```

```python
import functools
import math

import jax
import jax.numpy as jnp
from jax import lax
from jax.experimental import pallas as pl
from jax.experimental.pallas import tpu as pltpu
from jax.sharding import PartitionSpec as P

HD = 128
NSCHED = 12
MESH = pl.DeviceIdType.MESH

shift_factor = 5.0
norm_eps = 1e-06


def noise_level(level_index):
    fraction = level_index / NSCHED
    return shift_factor * fraction / (1.0 + (shift_factor - 1.0) * fraction)


def token_terms(steps_row, frame_index, freq):
    frame_count = steps_row.shape[0]
    hit = frame_index[:, None] == jnp.arange(frame_count, dtype=jnp.int32)[None, :]
    level_index = jnp.sum(jnp.where(hit, steps_row[None, :], 0), axis=1).astype(jnp.float32)
    upper = noise_level(level_index + 1.0)
    lower = noise_level(level_index)
    half_freq = freq // 2
    rates = jnp.exp(-math.log(10000.0) * jnp.arange(half_freq, dtype=jnp.float32) / half_freq)
    angles = (1000.0 * upper)[:, None] * rates[None, :]
    features = jnp.concatenate([jnp.cos(angles), jnp.sin(angles)], axis=1).astype(jnp.bfloat16)
    return features, (upper - lower)[:, None]


def kernel(
    tm_size, ctx_size,
    latent_ref, anchor_ref, feat_ref, gap_ref, frow_ref, qkv_ref, wo_ref, mod_ref,
    out_ref,
    wqkv, wo, wmod, own, buf, qbuf, acc, atts, attr, negate, drift, pdrift, xsend, xrecv, etot,
    w_sem, swap_send, swap_recv, ring_send, ring_recv, core_send, core_recv,
    att_send, att_recv, d_send, d_recv, x_send, x_recv, e_send, e_recv,
):
    R, D = latent_ref.shape[1], latent_ref.shape[2]
    half = D // 2
    Rp = own.shape[1]
    ring = ctx_size // 2
    pairs = tm_size // 2
    mid = ring // 2
    t = lax.axis_index("tm")
    c = lax.axis_index("ctx")
    a, k = t // 2, t % 2
    h, r = c // ring, c % ring
    u = r // 2
    p = 2 * u + (r % 2 + u) % 2

    def at_ring(q):
        v = q // 2
        return h * ring + 2 * v + (q % 2 + v) % 2

    core_peer = {"tm": 2 * a + 1 - k}
    swap_peer = {"tm": 2 * a + h, "ctx": k * ring + r}
    right = {"ctx": at_ring((p + 1) % ring)}
    left = {"ctx": at_ring((p + ring - 1) % ring)}

    loads = [pltpu.make_async_copy(mod_ref, wmod, w_sem.at[0])]
    for i in range(3):
        col = pl.multiple_of(i * D + k * half, 128)
        loads.append(pltpu.make_async_copy(qkv_ref.at[:, pl.ds(col, half)], wqkv.at[i], w_sem.at[1 + i]))
    loads.append(pltpu.make_async_copy(wo_ref, wo, w_sem.at[4]))
    for load in loads:
        load.start()

    barrier = pltpu.get_barrier_semaphore()
    greeted = [
        core_peer,
        {"tm": 2 * a + k, "ctx": (1 - h) * ring + r},
        {"tm": 2 * a + 1 - k, "ctx": (1 - h) * ring + r},
        left,
        right,
    ]
    for d in range(1, pairs):
        greeted.append({"tm": 2 * ((a + d) % pairs) + k})
    for peer in greeted:
        pl.semaphore_signal(barrier, inc=1, device_id=peer, device_id_type=MESH)

    x = latent_ref[0]
    center = x - jnp.mean(x, axis=-1, keepdims=True)
    spread = jnp.mean(center * center, axis=-1, keepdims=True)
    unit = center * lax.rsqrt(spread + norm_eps)
    loads[0].wait()
    feat = feat_ref[...]
    gap = gap_ref[...]
    for j in range(2):
        js = slice(j * half, (j + 1) * half)
        shift = jnp.dot(feat, wmod[:, j * half:(j + 1) * half], preferred_element_type=jnp.float32)
        scale = jnp.dot(feat, wmod[:, D + j * half:D + (j + 1) * half], preferred_element_type=jnp.float32)
        rows = unit[:, js] * (1.0 + scale) + shift
        tail = frow_ref[...] if j == 0 else jnp.zeros((Rp - R, half), jnp.float32)
        own[j] = jnp.concatenate([rows, tail], axis=0).astype(jnp.bfloat16)
    pl.semaphore_wait(barrier, len(greeted))

    def remote(src, dst, s_sem, r_sem, peer):
        return pltpu.make_async_remote_copy(
            src_ref=src, dst_ref=dst, send_sem=s_sem, recv_sem=r_sem, device_id=peer, device_id_type=MESH
        )

    def swap_copy(j):
        return remote(own.at[j], buf.at[0, j, h], swap_send.at[j], swap_recv.at[j], swap_peer)

    def swap_landed(j):
        return remote(own.at[j], buf.at[0, j, k], swap_send.at[j], swap_recv.at[j], swap_peer)

    @pl.when(k != h)
    def _():
        for j in range(2):
            swap_copy(j).start()

    @pl.when(k == h)
    def _():
        for j in range(2):
            buf[0, j, k] = own[j]

    @pl.when(k != h)
    def _():
        for j in range(2):
            swap_landed(j).wait_recv()

    def slot(way, s):
        if s == 0:
            return 0
        if s == mid:
            return mid
        return s if way == 0 else mid + s

    started = []

    def ring_copy(way, s, j):
        return remote(
            buf.at[slot(way, s), j, k], buf.at[slot(way, s + 1), j, k],
            ring_send.at[way, s, j], ring_recv.at[way, s, j], right if way == 0 else left,
        )

    def core_copy(sl, j):
        return remote(buf.at[sl, j, k], buf.at[sl, j, k], core_send.at[sl, j], core_recv.at[sl, j], core_peer)

    def start(copy):
        copy.start()
        started.append(copy)

    def core_wait(sl):
        for j in range(2):
            remote(
                buf.at[sl, j, 1 - k], buf.at[sl, j, 1 - k], core_send.at[sl, j], core_recv.at[sl, j], core_peer
            ).wait_recv()

    for step in range(2):
        for way in range(2):
            j = step if way == 0 else 1 - step
            if mid > 1 or step == 0:
                start(ring_copy(way, 0, j))
    for j in range(2):
        start(core_copy(0, j))

    for j in range(2):
        gate = jnp.dot(feat, wmod[:, 2 * D + j * half:2 * D + (j + 1) * half], preferred_element_type=jnp.float32)
        negate[j] = -gap * gate
        drift[j] = -gap * latent_ref[0, :, j * half:(j + 1) * half]

    score_scale = HD ** (-0.5) * math.log2(math.e)
    tiles = half // (2 * HD)
    n_rows = 2 * Rp

    def frames_of(sl):
        last = buf[sl, 0, 0, Rp - 16:Rp, :].astype(jnp.float32) + buf[sl, 0, 1, Rp - 16:Rp, :].astype(jnp.float32)
        place = R - (Rp - 16)
        return last[place:place + 1, :n_rows]

    def head_norm(rows):
        return (rows * lax.rsqrt(jnp.mean(rows * rows, axis=-1, keepdims=True) + norm_eps)).astype(jnp.bfloat16)

    def project(sl, i, j):
        cols = pl.ds(pl.multiple_of(j * 2 * HD, 2 * HD), 2 * HD)
        one = jnp.dot(
            buf[sl, 0].reshape(n_rows, half), wqkv[i, 0:half, cols], preferred_element_type=jnp.float32
        )
        return one + jnp.dot(
            buf[sl, 1].reshape(n_rows, half), wqkv[i, half:D, cols], preferred_element_type=jnp.float32
        )

    def attend(sl, query_frame):
        key_frame = frames_of(sl)
        ones = jnp.ones((n_rows, HD), jnp.bfloat16)

        def tile(j, carry):
            if sl == 0:
                qq = project(sl, 0, j)
                for g in range(2):
                    qbuf[j, g] = head_norm(qq[:, g * HD:(g + 1) * HD])
            kk = project(sl, 1, j)
            vv = project(sl, 2, j)
            allowed = key_frame <= query_frame
            for g in range(2):
                key = head_norm(kk[:, g * HD:(g + 1) * HD])
                value = jnp.concatenate([vv[:, g * HD:(g + 1) * HD].astype(jnp.bfloat16), ones], axis=1)
                scores = lax.dot_general(
                    qbuf[j, g], key, (((1,), (1,)), ((), ())), preferred_element_type=jnp.float32
                )
                weights = jnp.where(allowed, jnp.exp2(scores * score_scale), 0.0).astype(jnp.bfloat16)
                part = jnp.dot(weights, value, preferred_element_type=jnp.float32)
                if sl == 0:
                    acc[j, g] = part
                else:
                    acc[j, g] += part
            return carry

        lax.fori_loop(0, tiles, tile, 0)

    core_wait(0)
    own_frame = frames_of(0)
    diagonal = lax.broadcasted_iota(jnp.int32, (n_rows, n_rows), 0) == lax.broadcasted_iota(
        jnp.int32, (n_rows, n_rows), 1
    )
    query_frame = jnp.sum(jnp.where(diagonal, own_frame, 0.0), axis=1, keepdims=True)
    for i in range(3):
        loads[1 + i].wait()
    attend(0, query_frame)

    for s in range(1, mid + 1):
        for step in range(2):
            for way in range(2):
                j = step if way == 0 else 1 - step
                if s == mid and step == 1:
                    continue
                ring_copy(way, s - 1, j).wait_recv()
                if s < mid - 1 or (s == mid - 1 and step == 0):
                    start(ring_copy(way, s, j))
                start(core_copy(slot(way, s), j))
        if s < mid:
            for way in range(2):
                core_wait(slot(way, s))
                attend(slot(way, s), query_frame)
        else:
            core_wait(mid)
            attend(mid, query_frame)

    def att_copy(b):
        return remote(
            atts.at[b], attr.at[k], att_send.at[b], att_recv.at[k], {"tm": 2 * a + h, "ctx": b * ring + r}
        )

    for b in range(2):
        for j in range(tiles):
            for g in range(2):
                top = acc[j, g, b * Rp:(b + 1) * Rp, 0:HD]
                bottom = acc[j, g, b * Rp:(b + 1) * Rp, HD:2 * HD]
                first = (2 * j + g) * HD
                atts[b, :, first:first + HD] = (top / bottom).astype(jnp.bfloat16)
        mine = jnp.logical_and(k == h, k == b)

        @pl.when(mine)
        def _():
            attr[k] = atts[b]

        @pl.when(jnp.logical_not(mine))
        def _():
            att_copy(b).start()

    for i in range(2):
        @pl.when(jnp.logical_not(jnp.logical_and(k == h, k == i)))
        def _():
            remote(
                atts.at[i], attr.at[i], att_send.at[i], att_recv.at[i], {"tm": 2 * a + i, "ctx": k * ring + r}
            ).wait_recv()

    loads[4].wait()
    for j in range(2):
        branch = jnp.zeros((Rp, half), jnp.float32)
        for i in range(2):
            branch += jnp.dot(
                attr[i], wo[i * half:(i + 1) * half, j * half:(j + 1) * half], preferred_element_type=jnp.float32
            )
        drift[j] += negate[j] * branch[:R]
        start(remote(drift.at[j], pdrift.at[j], d_send.at[j], d_recv.at[j], core_peer))
    for j in range(2):
        remote(drift.at[j], pdrift.at[j], d_send.at[j], d_recv.at[j], core_peer).wait_recv()

    def x_copy(d):
        return remote(xsend, xrecv.at[d - 1], x_send.at[d - 1], x_recv.at[d - 1], {"tm": 2 * ((a + d) % pairs) + k})

    xsend[...] = drift[k] + pdrift[k]
    for d in range(1, pairs):
        @pl.when(a + d < pairs)
        def _():
            x_copy(d).start()

    e_copy = remote(etot.at[k], etot.at[k], e_send, e_recv, core_peer)
    e_landed = remote(etot.at[1 - k], etot.at[1 - k], e_send, e_recv, core_peer)
    for j in range(2):
        js = slice(j * half, (j + 1) * half)
        here = anchor_ref[:, js] + drift[j]
        out_ref[0, :, js] = jnp.where(k == 1, here + pdrift[j], here)

    @pl.when(a > 0)
    def _():
        etot[k] = jnp.zeros((R, half), jnp.float32)

    for d in range(1, pairs):
        @pl.when(a >= d)
        def _():
            x_copy(d).wait_recv()
            etot[k] += xrecv[d - 1]

    @pl.when(a > 0)
    def _():
        e_copy.start()
        e_landed.wait_recv()
        for j in range(2):
            js = slice(j * half, (j + 1) * half)
            out_ref[0, :, js] += etot[j]
        e_copy.wait_send()

    for copy in started:
        copy.wait_send()

    @pl.when(k != h)
    def _():
        for j in range(2):
            swap_copy(j).wait_send()

    for b in range(2):
        @pl.when(jnp.logical_not(jnp.logical_and(k == h, k == b)))
        def _():
            att_copy(b).wait_send()

    for d in range(1, pairs):
        @pl.when(a + d < pairs)
        def _():
            x_copy(d).wait_send()


def per_device(tm_size, ctx_size, iterate, anchor, frame_index, noise_steps, qkv_weight, out_weight, mod_weight):
    R, D = anchor.shape
    half = D // 2
    ring = ctx_size // 2
    pairs = tm_size // 2
    mid = ring // 2
    Rp = (R + 1 + 15) // 16 * 16
    features, gap = token_terms(noise_steps[0], frame_index, mod_weight.shape[0])
    never = float(4 * noise_steps.shape[1])
    frames = jnp.concatenate([frame_index.astype(jnp.float32), jnp.full((Rp - R,), never, jnp.float32)])
    zero = jnp.zeros_like(frames)
    high = lax.axis_index("ctx") // ring
    pair_row = jnp.concatenate([jnp.where(high == 0, frames, zero), jnp.where(high == 1, frames, zero)])
    frame_rows = jnp.pad(pair_row[None, :], ((0, Rp - R - 1), (0, half - 2 * Rp)))
    vmem = pl.BlockSpec(memory_space=pltpu.VMEM)
    hbm = pl.BlockSpec(memory_space=pl.ANY)
    dma = pltpu.SemaphoreType.DMA
    return pl.pallas_call(
        functools.partial(kernel, tm_size, ctx_size),
        out_shape=jax.ShapeDtypeStruct((1, R, D), jnp.float32),
        in_specs=[vmem] * 5 + [hbm] * 3,
        out_specs=vmem,
        scratch_shapes=[
            pltpu.VMEM((3, D, half), jnp.bfloat16),
            pltpu.VMEM((D, D), jnp.bfloat16),
            pltpu.VMEM(mod_weight.shape, jnp.bfloat16),
            pltpu.VMEM((2, Rp, half), jnp.bfloat16),
            pltpu.VMEM((ring, 2, 2, Rp, half), jnp.bfloat16),
            pltpu.VMEM((half // (2 * HD), 2, 2 * Rp, HD), jnp.bfloat16),
            pltpu.VMEM((half // (2 * HD), 2, 2 * Rp, 2 * HD), jnp.float32),
            pltpu.VMEM((2, Rp, half), jnp.bfloat16),
            pltpu.VMEM((2, Rp, half), jnp.bfloat16),
            pltpu.VMEM((2, R, half), jnp.float32),
            pltpu.VMEM((2, R, half), jnp.float32),
            pltpu.VMEM((2, R, half), jnp.float32),
            pltpu.VMEM((R, half), jnp.float32),
            pltpu.VMEM((max(pairs - 1, 1), R, half), jnp.float32),
            pltpu.VMEM((2, R, half), jnp.float32),
            dma((5,)),
            dma((2,)), dma((2,)),
            dma((2, mid, 2)), dma((2, mid, 2)),
            dma((ring, 2)), dma((ring, 2)),
            dma((2,)), dma((2,)),
            dma((2,)), dma((2,)),
            dma((max(pairs - 1, 1),)), dma((max(pairs - 1, 1),)),
            dma, dma,
        ],
        compiler_params=pltpu.CompilerParams(
            collective_id=0, has_side_effects=True, vmem_limit_bytes=56 * 1024 * 1024
        ),
    )(iterate, anchor, features, gap, frame_rows, qkv_weight, out_weight, mod_weight)


def solution(mesh):
    placed = (P("tm", "ctx", None), P("ctx", None), P("ctx"), P("tm", None), P(), P(), P())
    return jax.shard_map(
        functools.partial(per_device, mesh.shape["tm"], mesh.shape["ctx"]),
        mesh=mesh, in_specs=placed, out_specs=P("tm", "ctx", None), check_vma=False,
    )
```

```python
import functools
import math

import jax
import jax.numpy as jnp
from jax import lax
from jax.experimental import pallas as pl
from jax.experimental.pallas import tpu as pltpu
from jax.sharding import PartitionSpec as P

HD = 128
NSCHED = 12
MESH = pl.DeviceIdType.MESH

shift_factor = 5.0
norm_eps = 1e-06


def noise_level(level_index):
    fraction = level_index / NSCHED
    return shift_factor * fraction / (1.0 + (shift_factor - 1.0) * fraction)


def token_terms(steps_row, frame_index, freq):
    frame_count = steps_row.shape[0]
    hit = frame_index[:, None] == jnp.arange(frame_count, dtype=jnp.int32)[None, :]
    level_index = jnp.sum(jnp.where(hit, steps_row[None, :], 0), axis=1).astype(jnp.float32)
    upper = noise_level(level_index + 1.0)
    lower = noise_level(level_index)
    half_freq = freq // 2
    rates = jnp.exp(-math.log(10000.0) * jnp.arange(half_freq, dtype=jnp.float32) / half_freq)
    angles = (1000.0 * upper)[:, None] * rates[None, :]
    features = jnp.concatenate([jnp.cos(angles), jnp.sin(angles)], axis=1).astype(jnp.bfloat16)
    return features, (upper - lower)[:, None]


CHUNKS = 3


def kernel(
    tm_size, ctx_size,
    latent_ref, feat_ref, gap_ref, frow_ref, qkv_ref, wo_ref, mod_ref,
    out_ref,
    wqkv, wo, wmod, own, buf, qbuf, qframe, acc, kbuf, vbuf, atts, attr, negate, local, plocal, base, drift,
    db, pdb, xa, xar, yar, xs, xr, yr,
    w_sem, swap_send, swap_recv, ring_send, ring_recv, opp_send, opp_recv, core_send, core_recv,
    att_send, att_recv, n_send, n_recv, d_send, d_recv, xa_send, xa_recv, ya_send, ya_recv,
    x_send, x_recv, y_send, y_recv,
):
    R, D = latent_ref.shape[1], latent_ref.shape[2]
    half = D // 2
    wide = D // CHUNKS
    Rp = own.shape[1]
    ring = ctx_size // 2
    pairs = tm_size // 2
    mid = ring // 2
    t = lax.axis_index("tm")
    c = lax.axis_index("ctx")
    a, k = t // 2, t % 2
    h, r = c // ring, c % ring
    u = r // 2
    p = 2 * u + (r % 2 + u) % 2

    def at_ring(q):
        v = q // 2
        return h * ring + 2 * v + (q % 2 + v) % 2

    core_peer = {"tm": 2 * a + 1 - k}
    swap_peer = {"tm": 2 * a + h, "ctx": k * ring + r}
    right = {"ctx": at_ring((p + 1) % ring)}
    left = {"ctx": at_ring((p + ring - 1) % ring)}
    pair_peer = {"ctx": at_ring(p + 1 - 2 * (p % 2))}

    loads = [pltpu.make_async_copy(mod_ref, wmod, w_sem.at[0])]
    for i in range(3):
        col = pl.multiple_of(i * D + k * half, 128)
        loads.append(pltpu.make_async_copy(qkv_ref.at[:, pl.ds(col, half)], wqkv.at[i], w_sem.at[1 + i]))
    loads.append(pltpu.make_async_copy(wo_ref, wo, w_sem.at[4]))
    for load in loads:
        load.start()

    barrier = pltpu.get_barrier_semaphore()
    greeted = [
        core_peer,
        {"tm": 2 * a + k, "ctx": (1 - h) * ring + r},
        {"tm": 2 * a + 1 - k, "ctx": (1 - h) * ring + r},
        left,
        right,
    ]
    for d in range(1, pairs):
        greeted.append({"tm": 2 * ((a + d) % pairs) + k})
    for peer in greeted:
        pl.semaphore_signal(barrier, inc=1, device_id=peer, device_id_type=MESH)

    def remote(src, dst, s_sem, r_sem, peer):
        return pltpu.make_async_remote_copy(
            src_ref=src, dst_ref=dst, send_sem=s_sem, recv_sem=r_sem, device_id=peer, device_id_type=MESH
        )

    started = []

    def start(copy):
        copy.start()
        started.append(copy)

    def swap_copy(j):
        return remote(own.at[j], buf.at[0, j, h], swap_send.at[j], swap_recv.at[j], swap_peer)

    def swap_landed(j):
        return remote(own.at[j], buf.at[0, j, k], swap_send.at[j], swap_recv.at[j], swap_peer)

    x = latent_ref[0]
    center = x - jnp.mean(x, axis=-1, keepdims=True)
    spread = jnp.mean(center * center, axis=-1, keepdims=True)
    unit = center * lax.rsqrt(spread + norm_eps)
    loads[0].wait()
    feat = feat_ref[...]
    gap = gap_ref[...]
    for j in range(CHUNKS):
        lo, hi = j * wide, (j + 1) * wide
        shift = jnp.dot(feat, wmod[:, lo:hi], preferred_element_type=jnp.float32)
        scale = jnp.dot(feat, wmod[:, D + lo:D + hi], preferred_element_type=jnp.float32)
        rows = unit[:, lo:hi] * (1.0 + scale[:R]) + shift[:R]
        tail = frow_ref[...] if j == 0 else jnp.zeros((Rp - R, wide), jnp.float32)
        own[j] = jnp.concatenate([rows, tail], axis=0).astype(jnp.bfloat16)
        if j == 0:
            pl.semaphore_wait(barrier, len(greeted))

        @pl.when(k != h)
        def _():
            swap_copy(j).start()

        @pl.when(k == h)
        def _():
            buf[0, j, k] = own[j]

    def slot(way, s):
        if s == 0:
            return 0
        if s == mid:
            return mid
        return s if way == 0 else mid + s

    def ring_copy(way, s, j):
        return remote(
            buf.at[slot(way, s), j, k], buf.at[slot(way, s + 1), j, k],
            ring_send.at[way, s, j], ring_recv.at[way, s, j], right if way == 0 else left,
        )

    def opposite_copy():
        source = jnp.where(p % 2 == 0, slot(0, mid - 1), slot(1, mid - 1))
        return remote(buf.at[source, 1, k], buf.at[mid, 1, k], opp_send, opp_recv, pair_peer)

    def core_copy(sl, j):
        return remote(buf.at[sl, j, k], buf.at[sl, j, k], core_send.at[sl, j], core_recv.at[sl, j], core_peer)

    def core_wait(sl):
        for j in range(CHUNKS):
            remote(
                buf.at[sl, j, 1 - k], buf.at[sl, j, 1 - k], core_send.at[sl, j], core_recv.at[sl, j], core_peer
            ).wait_recv()

    for j in range(2):
        local[j] = -gap[:R] * latent_ref[0, :, j * half:(j + 1) * half]
        start(remote(local.at[j], plocal.at[j], n_send.at[j], n_recv.at[j], core_peer))

    for j in range(CHUNKS):
        @pl.when(k != h)
        def _():
            swap_landed(j).wait_recv()

        for way in range(2):
            start(ring_copy(way, 0, j))
        start(core_copy(0, j))

    for j in range(2):
        gate = jnp.dot(feat, wmod[:, 2 * D + j * half:2 * D + (j + 1) * half], preferred_element_type=jnp.float32)
        negate[j] = -gap * gate

    score_scale = HD ** (-0.5) * math.log2(math.e)
    tiles = half // (2 * HD)
    n_rows = 2 * Rp

    def frames_of(sl):
        last = buf[sl, 0, 0, Rp - 16:Rp, :].astype(jnp.float32) + buf[sl, 0, 1, Rp - 16:Rp, :].astype(jnp.float32)
        place = R - (Rp - 16)
        return last[place:place + 1, :n_rows]

    def head_norm(rows):
        return (rows * lax.rsqrt(jnp.mean(rows * rows, axis=-1, keepdims=True) + norm_eps)).astype(jnp.bfloat16)

    def project(sl, i, j):
        cols = pl.ds(pl.multiple_of(j * 2 * HD, 2 * HD), 2 * HD)
        total = None
        for m in range(CHUNKS):
            one = jnp.dot(
                buf[sl, m].reshape(n_rows, wide), wqkv[i, m * wide:(m + 1) * wide, cols],
                preferred_element_type=jnp.float32,
            )
            total = one if total is None else total + one
        return total

    def keys_values(sl, j):
        kk = project(sl, 1, j)
        vv = project(sl, 2, j)
        ones = jnp.ones((n_rows, HD), jnp.bfloat16)
        keys = [head_norm(kk[:, g * HD:(g + 1) * HD]) for g in range(2)]
        values = [
            jnp.concatenate([vv[:, g * HD:(g + 1) * HD].astype(jnp.bfloat16), ones], axis=1) for g in range(2)
        ]
        return keys, values

    def partial_sums(query, key, value, allowed):
        scores = lax.dot_general(query, key, (((1,), (1,)), ((), ())), preferred_element_type=jnp.float32)
        weights = jnp.where(allowed, jnp.exp2(scores * score_scale), 0.0).astype(jnp.bfloat16)
        return jnp.dot(weights, value, preferred_element_type=jnp.float32)

    def attend(sl):
        key_frame = frames_of(sl)

        def tile(j, carry):
            if sl == 0:
                qq = project(sl, 0, j)
                for g in range(2):
                    qbuf[j, g] = head_norm(qq[:, g * HD:(g + 1) * HD]).reshape(2, Rp, HD)
            keys, values = keys_values(sl, j)
            allowed = key_frame <= qframe[...].reshape(n_rows, 1)
            for g in range(2):
                part = partial_sums(qbuf[j, g].reshape(n_rows, HD), keys[g], values[g], allowed)
                part = part.reshape(2, Rp, 2 * HD)
                if sl == 0:
                    acc[j, g] = part
                else:
                    acc[j, g] += part
            return carry

        lax.fori_loop(0, tiles, tile, 0)

    core_wait(0)
    diagonal = lax.broadcasted_iota(jnp.int32, (n_rows, n_rows), 0) == lax.broadcasted_iota(
        jnp.int32, (n_rows, n_rows), 1
    )
    qframe[...] = jnp.sum(jnp.where(diagonal, frames_of(0), 0.0), axis=1, keepdims=True).reshape(2, Rp, 1)
    for i in range(3):
        loads[1 + i].wait()
    attend(0)

    def later(d):
        return {"tm": 2 * ((a + d) % pairs) + k}

    def xa_copy(d):
        return remote(xa, xar.at[d - 1], xa_send.at[d - 1], xa_recv.at[d - 1], later(d))

    def ya_copy(d):
        return remote(xar.at[d - 1], yar.at[d - 1], ya_send.at[d - 1], ya_recv.at[d - 1], core_peer)

    def x_copy(d):
        return remote(xs, xr.at[d - 1], x_send.at[d - 1], x_recv.at[d - 1], later(d))

    def y_copy(d):
        return remote(xr.at[d - 1], yr.at[d - 1], y_send.at[d - 1], y_recv.at[d - 1], core_peer)

    for j in range(2):
        remote(local.at[j], plocal.at[j], n_send.at[j], n_recv.at[j], core_peer).wait_recv()
    xa[...] = local[k] + plocal[k]
    for d in range(1, pairs):
        @pl.when(a + d < pairs)
        def _():
            xa_copy(d).start()

    for j in range(2):
        base[j] = jnp.where(k == 1, local[j] + plocal[j], local[j])

    for s in range(1, mid):
        for j in range(CHUNKS):
            for way in range(2):
                ring_copy(way, s - 1, j).wait_recv()
                if s < mid - 1 or (way == 0 and j == 0) or (way == 1 and j == CHUNKS - 1):
                    start(ring_copy(way, s, j))
                start(core_copy(slot(way, s), j))
            if s == mid - 1 and j == 1:
                start(opposite_copy())
        for way in range(2):
            core_wait(slot(way, s))
            attend(slot(way, s))

    for d in range(1, pairs):
        @pl.when(a >= d)
        def _():
            xa_copy(d).wait_recv()
            ya_copy(d).start()

    ring_copy(0, mid - 1, 0).wait_recv()
    start(core_copy(mid, 0))
    opposite_copy().wait_recv()
    start(core_copy(mid, 1))
    ring_copy(1, mid - 1, CHUNKS - 1).wait_recv()
    start(core_copy(mid, CHUNKS - 1))
    core_wait(mid)

    def last_tile(j, carry):
        keys, values = keys_values(mid, j)
        for g in range(2):
            kbuf[j, g] = keys[g]
            vbuf[j, g] = values[g]
        return carry

    lax.fori_loop(0, tiles, last_tile, 0)
    last_frame = frames_of(mid)

    def finish(b, m):
        allowed = last_frame <= qframe[b]
        for j in range(tiles):
            for g in range(2):
                full = acc[j, g, b] + partial_sums(qbuf[j, g, b], kbuf[j, g], vbuf[j, g], allowed)
                first = (2 * j + g) * HD
                atts[m, :, first:first + HD] = (full[:, :HD] / full[:, HD:]).astype(jnp.bfloat16)

    away = remote(
        atts.at[0], attr.at[k], att_send.at[0], att_recv.at[k], {"tm": 2 * a + h, "ctx": (1 - h) * ring + r}
    )
    across = remote(atts.at[1], attr.at[k], att_send.at[1], att_recv.at[k], core_peer)
    finish(1 - h, 0)
    start(away)
    finish(h, 1)

    @pl.when(k == h)
    def _():
        attr[k] = atts[1]

    @pl.when(k != h)
    def _():
        across.start()

    for d in range(1, pairs):
        @pl.when(a >= d)
        def _():
            ya_copy(d).wait_recv()
            base[k] += xar[d - 1]
            base[1 - k] += yar[d - 1]

    for i in range(2):
        @pl.when(jnp.logical_not(jnp.logical_and(k == h, k == i)))
        def _():
            remote(
                atts.at[i], attr.at[i], att_send.at[i], att_recv.at[i], {"tm": 2 * a + i, "ctx": k * ring + r}
            ).wait_recv()

    loads[4].wait()
    for j in range(2):
        branch = jnp.zeros((Rp, half), jnp.float32)
        for i in range(2):
            branch += jnp.dot(
                attr[i], wo[i * half:(i + 1) * half, j * half:(j + 1) * half], preferred_element_type=jnp.float32
            )
        drift[j] = negate[j] * branch
        db[j] = drift[j].astype(jnp.bfloat16)
        start(remote(db.at[j], pdb.at[j], d_send.at[j], d_recv.at[j], core_peer))
    for j in range(2):
        remote(db.at[j], pdb.at[j], d_send.at[j], d_recv.at[j], core_peer).wait_recv()

    xs[...] = (drift[k] + pdb[k].astype(jnp.float32)).astype(jnp.bfloat16)
    for d in range(1, pairs):
        @pl.when(a + d < pairs)
        def _():
            x_copy(d).start()

    for j in range(2):
        here = base[j] + drift[j, :R]
        base[j] = jnp.where(k == 1, here + pdb[j].astype(jnp.float32)[:R], here)

    for d in range(1, pairs):
        @pl.when(a >= d)
        def _():
            x_copy(d).wait_recv()
            y_copy(d).start()
            base[k] += xr[d - 1].astype(jnp.float32)[:R]
            y_copy(d).wait_recv()
            base[1 - k] += yr[d - 1].astype(jnp.float32)[:R]

    for j in range(2):
        out_ref[0, :, j * half:(j + 1) * half] = base[j]

    for copy in started:
        copy.wait_send()

    @pl.when(k != h)
    def _():
        for j in range(CHUNKS):
            swap_copy(j).wait_send()
        across.wait_send()

    for d in range(1, pairs):
        @pl.when(a + d < pairs)
        def _():
            xa_copy(d).wait_send()
            x_copy(d).wait_send()

        @pl.when(a >= d)
        def _():
            ya_copy(d).wait_send()
            y_copy(d).wait_send()


def per_device(tm_size, ctx_size, iterate, anchor, frame_index, noise_steps, qkv_weight, out_weight, mod_weight):
    R, D = anchor.shape
    half = D // 2
    wide = D // CHUNKS
    ring = ctx_size // 2
    pairs = tm_size // 2
    far = max(pairs - 1, 1)
    mid = ring // 2
    Rp = (R + 1 + 15) // 16 * 16
    tiles = half // (2 * HD)
    features, gap = token_terms(noise_steps[0], frame_index, mod_weight.shape[0])
    features = jnp.pad(features, ((0, Rp - R), (0, 0)))
    gap = jnp.pad(gap, ((0, Rp - R), (0, 0)))
    never = float(4 * noise_steps.shape[1])
    frames = jnp.concatenate([frame_index.astype(jnp.float32), jnp.full((Rp - R,), never, jnp.float32)])
    zero = jnp.zeros_like(frames)
    high = lax.axis_index("ctx") // ring
    pair_row = jnp.concatenate([jnp.where(high == 0, frames, zero), jnp.where(high == 1, frames, zero)])
    frame_rows = jnp.pad(pair_row[None, :], ((0, Rp - R - 1), (0, wide - 2 * Rp)))
    vmem = pl.BlockSpec(memory_space=pltpu.VMEM)
    hbm = pl.BlockSpec(memory_space=pl.ANY)
    dma = pltpu.SemaphoreType.DMA
    f32, bf16 = jnp.float32, jnp.bfloat16
    total = pl.pallas_call(
        functools.partial(kernel, tm_size, ctx_size),
        out_shape=jax.ShapeDtypeStruct((1, R, D), f32),
        in_specs=[vmem] * 4 + [hbm] * 3,
        out_specs=vmem,
        scratch_shapes=[
            pltpu.VMEM((3, D, half), bf16),
            pltpu.VMEM((D, D), bf16),
            pltpu.VMEM(mod_weight.shape, bf16),
            pltpu.VMEM((CHUNKS, Rp, wide), bf16),
            pltpu.VMEM((ring, CHUNKS, 2, Rp, wide), bf16),
            pltpu.VMEM((tiles, 2, 2, Rp, HD), bf16),
            pltpu.VMEM((2, Rp, 1), f32),
            pltpu.VMEM((tiles, 2, 2, Rp, 2 * HD), f32),
            pltpu.VMEM((tiles, 2, 2 * Rp, HD), bf16),
            pltpu.VMEM((tiles, 2, 2 * Rp, 2 * HD), bf16),
            pltpu.VMEM((2, Rp, half), bf16),
            pltpu.VMEM((2, Rp, half), bf16),
            pltpu.VMEM((2, Rp, half), f32),
            pltpu.VMEM((2, R, half), f32),
            pltpu.VMEM((2, R, half), f32),
            pltpu.VMEM((2, R, half), f32),
            pltpu.VMEM((2, Rp, half), f32),
            pltpu.VMEM((2, Rp, half), bf16),
            pltpu.VMEM((2, Rp, half), bf16),
            pltpu.VMEM((R, half), f32),
            pltpu.VMEM((far, R, half), f32),
            pltpu.VMEM((far, R, half), f32),
            pltpu.VMEM((Rp, half), bf16),
            pltpu.VMEM((far, Rp, half), bf16),
            pltpu.VMEM((far, Rp, half), bf16),
            dma((5,)),
            dma((CHUNKS,)), dma((CHUNKS,)),
            dma((2, mid, CHUNKS)), dma((2, mid, CHUNKS)),
            dma, dma,
            dma((ring, CHUNKS)), dma((ring, CHUNKS)),
            dma((2,)), dma((2,)),
            dma((2,)), dma((2,)),
            dma((2,)), dma((2,)),
            dma((far,)), dma((far,)),
            dma((far,)), dma((far,)),
            dma((far,)), dma((far,)),
            dma((far,)), dma((far,)),
        ],
        compiler_params=pltpu.CompilerParams(
            collective_id=0, has_side_effects=True, vmem_limit_bytes=56 * 1024 * 1024
        ),
    )(iterate, features, gap, frame_rows, qkv_weight, out_weight, mod_weight)
    return anchor[None] + total


def solution(mesh):
    placed = (P("tm", "ctx", None), P("ctx", None), P("ctx"), P("tm", None), P(), P(), P())
    return jax.shard_map(
        functools.partial(per_device, mesh.shape["tm"], mesh.shape["ctx"]),
        mesh=mesh, in_specs=placed, out_specs=P("tm", "ctx", None), check_vma=False,
    )
```

```python
import functools
import math

import jax
import jax.numpy as jnp
from jax import lax
from jax.experimental import pallas as pl
from jax.experimental.pallas import tpu as pltpu
from jax.sharding import PartitionSpec as P

HD = 128
NSCHED = 12
MESH = pl.DeviceIdType.MESH

shift_factor = 5.0
norm_eps = 1e-06


def noise_level(level_index):
    fraction = level_index / NSCHED
    return shift_factor * fraction / (1.0 + (shift_factor - 1.0) * fraction)


CHUNKS = 3


def kernel(
    tm_size, ctx_size,
    latent_ref, frame_ref, steps_ref, qkv_ref, wo_ref, mod_ref,
    out_ref,
    wqkv, wo, wmod, own, buf, qbuf, qframe, acc, kbuf, vbuf, atts, attr, negate, local, plocal, base, drift,
    db, pdb, xa, xar, yar, xs, xr, yr,
    w_sem, swap_send, swap_recv, ring_send, ring_recv, opp_send, opp_recv, core_send, core_recv,
    att_send, att_recv, n_send, n_recv, d_send, d_recv, xa_send, xa_recv, ya_send, ya_recv,
    x_send, x_recv, y_send, y_recv,
):
    R, D = latent_ref.shape[1], latent_ref.shape[2]
    half = D // 2
    wide = D // CHUNKS
    Rp = own.shape[1]
    ring = ctx_size // 2
    pairs = tm_size // 2
    mid = ring // 2
    t = lax.axis_index("tm")
    c = lax.axis_index("ctx")
    a, k = t // 2, t % 2
    h, r = c // ring, c % ring
    u = r // 2
    p = 2 * u + (r % 2 + u) % 2

    def at_ring(q):
        v = q // 2
        return h * ring + 2 * v + (q % 2 + v) % 2

    core_peer = {"tm": 2 * a + 1 - k}
    swap_peer = {"tm": 2 * a + h, "ctx": k * ring + r}
    right = {"ctx": at_ring((p + 1) % ring)}
    left = {"ctx": at_ring((p + ring - 1) % ring)}
    pair_peer = {"ctx": at_ring(p + 1 - 2 * (p % 2))}

    loads = [pltpu.make_async_copy(mod_ref, wmod, w_sem.at[0])]
    for i in range(3):
        col = pl.multiple_of(i * D + k * half, 128)
        loads.append(pltpu.make_async_copy(qkv_ref.at[:, pl.ds(col, half)], wqkv.at[i], w_sem.at[1 + i]))
    loads.append(pltpu.make_async_copy(wo_ref, wo, w_sem.at[4]))
    loads[0].start()

    barrier = pltpu.get_barrier_semaphore()
    greeted = [
        core_peer,
        {"tm": 2 * a + k, "ctx": (1 - h) * ring + r},
        {"tm": 2 * a + 1 - k, "ctx": (1 - h) * ring + r},
        left,
        right,
    ]
    for d in range(1, pairs):
        greeted.append({"tm": 2 * ((a + d) % pairs) + k})
    for peer in greeted:
        pl.semaphore_signal(barrier, inc=1, device_id=peer, device_id_type=MESH)

    def remote(src, dst, s_sem, r_sem, peer):
        return pltpu.make_async_remote_copy(
            src_ref=src, dst_ref=dst, send_sem=s_sem, recv_sem=r_sem, device_id=peer, device_id_type=MESH
        )

    started = []

    def start(copy):
        copy.start()
        started.append(copy)

    def swap_copy(j):
        return remote(own.at[j], buf.at[0, j, h], swap_send.at[j], swap_recv.at[j], swap_peer)

    def swap_landed(j):
        return remote(own.at[j], buf.at[0, j, k], swap_send.at[j], swap_recv.at[j], swap_peer)

    x = latent_ref[0]
    center = x - jnp.mean(x, axis=-1, keepdims=True)
    spread = jnp.mean(center * center, axis=-1, keepdims=True)
    unit = center * lax.rsqrt(spread + norm_eps)

    row_place = lax.broadcasted_iota(jnp.int32, (Rp, R), 0)
    lane_place = lax.broadcasted_iota(jnp.int32, (Rp, R), 1)
    frame_row = frame_ref[...].astype(jnp.float32)
    frame_col = jnp.sum(jnp.where(row_place == lane_place, frame_row, 0.0), axis=1, keepdims=True)
    level_index = jnp.zeros((Rp, 1), jnp.float32)
    for f in range(steps_ref.shape[1]):
        level_index += jnp.where(frame_col == float(f), steps_ref[0, f].astype(jnp.float32), 0.0)
    upper = noise_level(level_index + 1.0)
    gap = upper - noise_level(level_index)
    half_freq = mod_ref.shape[0] // 2
    rate_place = lax.broadcasted_iota(jnp.int32, (1, half_freq), 1).astype(jnp.float32)
    rates = jnp.exp(-math.log(10000.0) * rate_place / half_freq)
    angles = (1000.0 * upper) * rates
    feat = jnp.concatenate([jnp.cos(angles), jnp.sin(angles)], axis=1).astype(jnp.bfloat16)
    here_row = lax.broadcasted_iota(jnp.int32, (Rp, wide), 0)
    here_lane = lax.broadcasted_iota(jnp.int32, (Rp, wide), 1)
    never = float(4 * steps_ref.shape[1])
    told = jnp.where(here_row < R, frame_col, never)
    frames_out = jnp.sum(jnp.where(here_lane == here_row + h * Rp, told, 0.0), axis=0, keepdims=True)
    spare_row = lax.broadcasted_iota(jnp.int32, (Rp - R, wide), 0)
    frames_tail = jnp.where(spare_row == 0, frames_out, 0.0)

    loads[0].wait()
    for load in loads[1:]:
        load.start()
    for j in range(CHUNKS):
        lo, hi = j * wide, (j + 1) * wide
        shift = jnp.dot(feat, wmod[:, lo:hi], preferred_element_type=jnp.float32)
        scale = jnp.dot(feat, wmod[:, D + lo:D + hi], preferred_element_type=jnp.float32)
        rows = unit[:, lo:hi] * (1.0 + scale[:R]) + shift[:R]
        tail = frames_tail if j == 0 else jnp.zeros((Rp - R, wide), jnp.float32)
        own[j] = jnp.concatenate([rows, tail], axis=0).astype(jnp.bfloat16)
        if j == 0:
            pl.semaphore_wait(barrier, len(greeted))

        @pl.when(k != h)
        def _():
            swap_copy(j).start()

        @pl.when(k == h)
        def _():
            buf[0, j, k] = own[j]

    def slot(way, s):
        if s == 0:
            return 0
        if s == mid:
            return mid
        return s if way == 0 else mid + s

    def ring_copy(way, s, j):
        return remote(
            buf.at[slot(way, s), j, k], buf.at[slot(way, s + 1), j, k],
            ring_send.at[way, s, j], ring_recv.at[way, s, j], right if way == 0 else left,
        )

    def opposite_copy():
        source = jnp.where(p % 2 == 0, slot(0, mid - 1), slot(1, mid - 1))
        return remote(buf.at[source, 1, k], buf.at[mid, 1, k], opp_send, opp_recv, pair_peer)

    def core_copy(sl, j):
        return remote(buf.at[sl, j, k], buf.at[sl, j, k], core_send.at[sl, j], core_recv.at[sl, j], core_peer)

    def core_wait(sl):
        for j in range(CHUNKS):
            remote(
                buf.at[sl, j, 1 - k], buf.at[sl, j, 1 - k], core_send.at[sl, j], core_recv.at[sl, j], core_peer
            ).wait_recv()

    for j in range(2):
        local[j] = -gap[:R] * latent_ref[0, :, j * half:(j + 1) * half]
        start(remote(local.at[j], plocal.at[j], n_send.at[j], n_recv.at[j], core_peer))

    for j in range(CHUNKS):
        @pl.when(k != h)
        def _():
            swap_landed(j).wait_recv()

        for way in range(2):
            start(ring_copy(way, 0, j))
        start(core_copy(0, j))

    for j in range(2):
        gate = jnp.dot(feat, wmod[:, 2 * D + j * half:2 * D + (j + 1) * half], preferred_element_type=jnp.float32)
        negate[j] = -gap * gate

    score_scale = HD ** (-0.5) * math.log2(math.e)
    tiles = half // (2 * HD)
    n_rows = 2 * Rp

    def frames_of(sl):
        last = buf[sl, 0, 0, Rp - 16:Rp, :].astype(jnp.float32) + buf[sl, 0, 1, Rp - 16:Rp, :].astype(jnp.float32)
        place = R - (Rp - 16)
        return last[place:place + 1, :n_rows]

    def head_norm(rows):
        return (rows * lax.rsqrt(jnp.mean(rows * rows, axis=-1, keepdims=True) + norm_eps)).astype(jnp.bfloat16)

    def project(sl, i, j):
        cols = pl.ds(pl.multiple_of(j * 2 * HD, 2 * HD), 2 * HD)
        total = None
        for m in range(CHUNKS):
            one = jnp.dot(
                buf[sl, m].reshape(n_rows, wide), wqkv[i, m * wide:(m + 1) * wide, cols],
                preferred_element_type=jnp.float32,
            )
            total = one if total is None else total + one
        return total

    def keys_values(sl, j):
        kk = project(sl, 1, j)
        vv = project(sl, 2, j)
        ones = jnp.ones((n_rows, HD), jnp.bfloat16)
        keys = [head_norm(kk[:, g * HD:(g + 1) * HD]) for g in range(2)]
        values = [
            jnp.concatenate([vv[:, g * HD:(g + 1) * HD].astype(jnp.bfloat16), ones], axis=1) for g in range(2)
        ]
        return keys, values

    def partial_sums(query, key, value, allowed):
        scores = lax.dot_general(query, key, (((1,), (1,)), ((), ())), preferred_element_type=jnp.float32)
        weights = jnp.where(allowed, jnp.exp2(scores * score_scale), 0.0).astype(jnp.bfloat16)
        return jnp.dot(weights, value, preferred_element_type=jnp.float32)

    def attend(sl):
        key_frame = frames_of(sl)

        def tile(j, carry):
            if sl == 0:
                qq = project(sl, 0, j)
                for g in range(2):
                    qbuf[j, g] = head_norm(qq[:, g * HD:(g + 1) * HD]).reshape(2, Rp, HD)
            keys, values = keys_values(sl, j)
            allowed = key_frame <= qframe[...].reshape(n_rows, 1)
            for g in range(2):
                part = partial_sums(qbuf[j, g].reshape(n_rows, HD), keys[g], values[g], allowed)
                part = part.reshape(2, Rp, 2 * HD)
                if sl == 0:
                    acc[j, g] = part
                else:
                    acc[j, g] += part
            return carry

        lax.fori_loop(0, tiles, tile, 0)

    core_wait(0)
    diagonal = lax.broadcasted_iota(jnp.int32, (n_rows, n_rows), 0) == lax.broadcasted_iota(
        jnp.int32, (n_rows, n_rows), 1
    )
    qframe[...] = jnp.sum(jnp.where(diagonal, frames_of(0), 0.0), axis=1, keepdims=True).reshape(2, Rp, 1)
    for i in range(3):
        loads[1 + i].wait()
    attend(0)

    def later(d):
        return {"tm": 2 * ((a + d) % pairs) + k}

    def xa_copy(d):
        return remote(xa, xar.at[d - 1], xa_send.at[d - 1], xa_recv.at[d - 1], later(d))

    def ya_copy(d):
        return remote(xar.at[d - 1], yar.at[d - 1], ya_send.at[d - 1], ya_recv.at[d - 1], core_peer)

    first_rows = (Rp // 2 + 15) // 16 * 16
    bands = [(0, first_rows), (first_rows, Rp)]

    def band(ref, i):
        return ref.at[bands[i][0]:bands[i][1]]

    def x_copy(d, i):
        return remote(
            band(xs, i), band(xr.at[d - 1], i), x_send.at[d - 1, i], x_recv.at[d - 1, i], later(d)
        )

    def y_copy(d, i):
        return remote(
            band(xr.at[d - 1], i), band(yr.at[d - 1], i), y_send.at[d - 1, i], y_recv.at[d - 1, i], core_peer
        )

    for j in range(2):
        remote(local.at[j], plocal.at[j], n_send.at[j], n_recv.at[j], core_peer).wait_recv()
    xa[...] = local[k] + plocal[k]
    for d in range(1, pairs):
        @pl.when(a + d < pairs)
        def _():
            xa_copy(d).start()

    for j in range(2):
        base[j] = jnp.where(k == 1, local[j] + plocal[j], local[j])

    for s in range(1, mid):
        for j in range(CHUNKS):
            for way in range(2):
                ring_copy(way, s - 1, j).wait_recv()
                if s < mid - 1 or (way == 0 and j == 0) or (way == 1 and j == CHUNKS - 1):
                    start(ring_copy(way, s, j))
                start(core_copy(slot(way, s), j))
            if s == mid - 1 and j == 1:
                start(opposite_copy())
        for way in range(2):
            core_wait(slot(way, s))
            attend(slot(way, s))

    for d in range(1, pairs):
        @pl.when(a >= d)
        def _():
            xa_copy(d).wait_recv()
            ya_copy(d).start()

    ring_copy(0, mid - 1, 0).wait_recv()
    start(core_copy(mid, 0))
    opposite_copy().wait_recv()
    start(core_copy(mid, 1))
    ring_copy(1, mid - 1, CHUNKS - 1).wait_recv()
    start(core_copy(mid, CHUNKS - 1))
    core_wait(mid)

    def last_tile(j, carry):
        keys, values = keys_values(mid, j)
        for g in range(2):
            kbuf[j, g] = keys[g]
            vbuf[j, g] = values[g]
        return carry

    lax.fori_loop(0, tiles, last_tile, 0)
    last_frame = frames_of(mid)

    def finish(b, m, i):
        lo, hi = bands[i]
        allowed = last_frame <= qframe[b, lo:hi]
        for j in range(tiles):
            for g in range(2):
                part = partial_sums(qbuf[j, g, b, lo:hi], kbuf[j, g], vbuf[j, g], allowed)
                full = acc[j, g, b, lo:hi] + part
                first = (2 * j + g) * HD
                atts[m, lo:hi, first:first + HD] = (full[:, :HD] / full[:, HD:]).astype(jnp.bfloat16)

    def away(i):
        return remote(
            band(atts.at[0], i), band(attr.at[k], i), att_send.at[0, i], att_recv.at[k, i],
            {"tm": 2 * a + h, "ctx": (1 - h) * ring + r},
        )

    def across(i):
        return remote(
            band(atts.at[1], i), band(attr.at[k], i), att_send.at[1, i], att_recv.at[k, i], core_peer
        )

    for i in range(2):
        finish(1 - h, 0, i)
        start(away(i))
    for i in range(2):
        finish(h, 1, i)

        @pl.when(k != h)
        def _():
            across(i).start()

    @pl.when(k == h)
    def _():
        attr[k] = atts[1]

    for d in range(1, pairs):
        @pl.when(a >= d)
        def _():
            ya_copy(d).wait_recv()
            base[k] += xar[d - 1]
            base[1 - k] += yar[d - 1]

    loads[4].wait()

    def d_copy(j, i):
        return remote(band(db.at[j], i), band(pdb.at[j], i), d_send.at[j, i], d_recv.at[j, i], core_peer)

    for i in range(2):
        lo, hi = bands[i]
        for m in range(2):
            @pl.when(jnp.logical_not(jnp.logical_and(k == h, k == m)))
            def _():
                remote(
                    band(atts.at[m], i), band(attr.at[m], i), att_send.at[m, i], att_recv.at[m, i],
                    {"tm": 2 * a + m, "ctx": k * ring + r},
                ).wait_recv()

        for j in range(2):
            branch = jnp.zeros((hi - lo, half), jnp.float32)
            for m in range(2):
                branch += jnp.dot(
                    attr[m, lo:hi], wo[m * half:(m + 1) * half, j * half:(j + 1) * half],
                    preferred_element_type=jnp.float32,
                )
            drift[j, lo:hi] = negate[j, lo:hi] * branch
            db[j, lo:hi] = drift[j, lo:hi].astype(jnp.bfloat16)
            start(d_copy(j, i))
        for j in range(2):
            d_copy(j, i).wait_recv()
        xs[lo:hi] = (drift[k, lo:hi] + pdb[k, lo:hi].astype(jnp.float32)).astype(jnp.bfloat16)
        for d in range(1, pairs):
            @pl.when(a + d < pairs)
            def _():
                x_copy(d, i).start()

    for j in range(2):
        here = base[j] + drift[j, :R]
        base[j] = jnp.where(k == 1, here + pdb[j].astype(jnp.float32)[:R], here)

    for d in range(1, pairs):
        @pl.when(a >= d)
        def _():
            for i in range(2):
                x_copy(d, i).wait_recv()
                y_copy(d, i).start()
            base[k] += xr[d - 1].astype(jnp.float32)[:R]
            for i in range(2):
                y_copy(d, i).wait_recv()
            base[1 - k] += yr[d - 1].astype(jnp.float32)[:R]

    for j in range(2):
        out_ref[0, :, j * half:(j + 1) * half] = base[j]

    for copy in started:
        copy.wait_send()

    @pl.when(k != h)
    def _():
        for j in range(CHUNKS):
            swap_copy(j).wait_send()
        for i in range(2):
            across(i).wait_send()

    for d in range(1, pairs):
        @pl.when(a + d < pairs)
        def _():
            xa_copy(d).wait_send()
            for i in range(2):
                x_copy(d, i).wait_send()

        @pl.when(a >= d)
        def _():
            ya_copy(d).wait_send()
            for i in range(2):
                y_copy(d, i).wait_send()


def per_device(tm_size, ctx_size, iterate, anchor, frame_index, noise_steps, qkv_weight, out_weight, mod_weight):
    R, D = anchor.shape
    half = D // 2
    wide = D // CHUNKS
    ring = ctx_size // 2
    pairs = tm_size // 2
    far = max(pairs - 1, 1)
    mid = ring // 2
    Rp = (R + 1 + 15) // 16 * 16
    tiles = half // (2 * HD)
    vmem = pl.BlockSpec(memory_space=pltpu.VMEM)
    hbm = pl.BlockSpec(memory_space=pl.ANY)
    dma = pltpu.SemaphoreType.DMA
    f32, bf16 = jnp.float32, jnp.bfloat16
    total = pl.pallas_call(
        functools.partial(kernel, tm_size, ctx_size),
        out_shape=jax.ShapeDtypeStruct((1, R, D), f32),
        in_specs=[vmem, vmem, pl.BlockSpec(memory_space=pltpu.SMEM)] + [hbm] * 3,
        out_specs=vmem,
        scratch_shapes=[
            pltpu.VMEM((3, D, half), bf16),
            pltpu.VMEM((D, D), bf16),
            pltpu.VMEM(mod_weight.shape, bf16),
            pltpu.VMEM((CHUNKS, Rp, wide), bf16),
            pltpu.VMEM((ring, CHUNKS, 2, Rp, wide), bf16),
            pltpu.VMEM((tiles, 2, 2, Rp, HD), bf16),
            pltpu.VMEM((2, Rp, 1), f32),
            pltpu.VMEM((tiles, 2, 2, Rp, 2 * HD), f32),
            pltpu.VMEM((tiles, 2, 2 * Rp, HD), bf16),
            pltpu.VMEM((tiles, 2, 2 * Rp, 2 * HD), bf16),
            pltpu.VMEM((2, Rp, half), bf16),
            pltpu.VMEM((2, Rp, half), bf16),
            pltpu.VMEM((2, Rp, half), f32),
            pltpu.VMEM((2, R, half), f32),
            pltpu.VMEM((2, R, half), f32),
            pltpu.VMEM((2, R, half), f32),
            pltpu.VMEM((2, Rp, half), f32),
            pltpu.VMEM((2, Rp, half), bf16),
            pltpu.VMEM((2, Rp, half), bf16),
            pltpu.VMEM((R, half), f32),
            pltpu.VMEM((far, R, half), f32),
            pltpu.VMEM((far, R, half), f32),
            pltpu.VMEM((Rp, half), bf16),
            pltpu.VMEM((far, Rp, half), bf16),
            pltpu.VMEM((far, Rp, half), bf16),
            dma((5,)),
            dma((CHUNKS,)), dma((CHUNKS,)),
            dma((2, mid, CHUNKS)), dma((2, mid, CHUNKS)),
            dma, dma,
            dma((ring, CHUNKS)), dma((ring, CHUNKS)),
            dma((2, 2)), dma((2, 2)),
            dma((2,)), dma((2,)),
            dma((2, 2)), dma((2, 2)),
            dma((far,)), dma((far,)),
            dma((far,)), dma((far,)),
            dma((far, 2)), dma((far, 2)),
            dma((far, 2)), dma((far, 2)),
        ],
        compiler_params=pltpu.CompilerParams(
            collective_id=0, has_side_effects=True, vmem_limit_bytes=56 * 1024 * 1024
        ),
    )(iterate, frame_index[None, :], noise_steps, qkv_weight, out_weight, mod_weight)
    return anchor[None] + total


def solution(mesh):
    placed = (P("tm", "ctx", None), P("ctx", None), P("ctx"), P("tm", None), P(), P(), P())
    return jax.shard_map(
        functools.partial(per_device, mesh.shape["tm"], mesh.shape["ctx"]),
        mesh=mesh, in_specs=placed, out_specs=P("tm", "ctx", None), check_vma=False,
    )
```

```python
import functools
import math

import jax
import jax.numpy as jnp
from jax import lax
from jax.experimental import pallas as pl
from jax.experimental.pallas import tpu as pltpu
from jax.sharding import PartitionSpec as P

HD = 128
NSCHED = 12
MESH = pl.DeviceIdType.MESH

shift_factor = 5.0
norm_eps = 1e-06


def noise_level(level_index):
    fraction = level_index / NSCHED
    return shift_factor * fraction / (1.0 + (shift_factor - 1.0) * fraction)


CHUNKS = 3


def kernel(
    tm_size, ctx_size,
    latent_ref, frame_ref, steps_ref, qkv_ref, wo_ref, mod_ref,
    out_ref,
    wqkv, wo, wmod, own, buf, qbuf, qframe, acc, kbuf, vbuf, atts, attr, negate, local, plocal, base, drift,
    db, pdb, xa, xar, yar, xs, xr, yr,
    w_sem, swap_send, swap_recv, ring_send, ring_recv, opp_send, opp_recv, core_send, core_recv,
    att_send, att_recv, n_send, n_recv, d_send, d_recv, xa_send, xa_recv, ya_send, ya_recv,
    x_send, x_recv, y_send, y_recv,
):
    R, D = latent_ref.shape[1], latent_ref.shape[2]
    half = D // 2
    wide = D // CHUNKS
    Rp = own.shape[1]
    ring = ctx_size // 2
    pairs = tm_size // 2
    mid = ring // 2
    t = lax.axis_index("tm")
    c = lax.axis_index("ctx")
    a, k = t // 2, t % 2
    h, r = c // ring, c % ring
    u = r // 2
    p = 2 * u + (r % 2 + u) % 2

    def at_ring(q):
        v = q // 2
        return h * ring + 2 * v + (q % 2 + v) % 2

    core_peer = {"tm": 2 * a + 1 - k}
    swap_peer = {"tm": 2 * a + h, "ctx": k * ring + r}
    right = {"ctx": at_ring((p + 1) % ring)}
    left = {"ctx": at_ring((p + ring - 1) % ring)}
    pair_peer = {"ctx": at_ring(p + 1 - 2 * (p % 2))}

    loads = [pltpu.make_async_copy(mod_ref, wmod, w_sem.at[0])]
    for i in range(3):
        col = pl.multiple_of(i * D + k * half, 128)
        loads.append(pltpu.make_async_copy(qkv_ref.at[:, pl.ds(col, half)], wqkv.at[i], w_sem.at[1 + i]))
    loads.append(pltpu.make_async_copy(wo_ref, wo, w_sem.at[4]))
    loads[0].start()

    barrier = pltpu.get_barrier_semaphore()
    greeted = [
        core_peer,
        {"tm": 2 * a + k, "ctx": (1 - h) * ring + r},
        {"tm": 2 * a + 1 - k, "ctx": (1 - h) * ring + r},
        left,
        right,
    ]
    for d in range(1, pairs):
        greeted.append({"tm": 2 * ((a + d) % pairs) + k})
    for peer in greeted:
        pl.semaphore_signal(barrier, inc=1, device_id=peer, device_id_type=MESH)

    def remote(src, dst, s_sem, r_sem, peer):
        return pltpu.make_async_remote_copy(
            src_ref=src, dst_ref=dst, send_sem=s_sem, recv_sem=r_sem, device_id=peer, device_id_type=MESH
        )

    started = []

    def start(make, *what):
        make(*what).start()
        started.append((make, what))

    def swap_copy(j):
        return remote(own.at[j], buf.at[0, j, h], swap_send.at[j], swap_recv.at[j], swap_peer)

    def swap_landed(j):
        return remote(own.at[j], buf.at[0, j, k], swap_send.at[j], swap_recv.at[j], swap_peer)

    x = latent_ref[0]
    center = x - jnp.mean(x, axis=-1, keepdims=True)
    spread = jnp.mean(center * center, axis=-1, keepdims=True)
    unit = center * lax.rsqrt(spread + norm_eps)

    row_place = lax.broadcasted_iota(jnp.int32, (Rp, R), 0)
    lane_place = lax.broadcasted_iota(jnp.int32, (Rp, R), 1)
    frame_row = frame_ref[...].astype(jnp.float32)
    frame_col = jnp.sum(jnp.where(row_place == lane_place, frame_row, 0.0), axis=1, keepdims=True)
    level_index = jnp.zeros((Rp, 1), jnp.float32)
    for f in range(steps_ref.shape[1]):
        level_index += jnp.where(frame_col == float(f), steps_ref[0, f].astype(jnp.float32), 0.0)
    upper = noise_level(level_index + 1.0)
    gap = upper - noise_level(level_index)
    half_freq = mod_ref.shape[0] // 2
    rate_place = lax.broadcasted_iota(jnp.int32, (1, half_freq), 1).astype(jnp.float32)
    rates = jnp.exp(-math.log(10000.0) * rate_place / half_freq)
    angles = (1000.0 * upper) * rates
    feat = jnp.concatenate([jnp.cos(angles), jnp.sin(angles)], axis=1).astype(jnp.bfloat16)
    here_row = lax.broadcasted_iota(jnp.int32, (Rp, wide), 0)
    here_lane = lax.broadcasted_iota(jnp.int32, (Rp, wide), 1)
    never = float(4 * steps_ref.shape[1])
    told = jnp.where(here_row < R, frame_col, never)
    frames_out = jnp.sum(jnp.where(here_lane == here_row + h * Rp, told, 0.0), axis=0, keepdims=True)
    spare_row = lax.broadcasted_iota(jnp.int32, (Rp - R, wide), 0)
    frames_tail = jnp.where(spare_row == 0, frames_out, 0.0)

    loads[0].wait()
    for load in loads[1:]:
        load.start()
    for j in range(CHUNKS):
        lo, hi = j * wide, (j + 1) * wide
        shift = jnp.dot(feat, wmod[:, lo:hi], preferred_element_type=jnp.float32)
        scale = jnp.dot(feat, wmod[:, D + lo:D + hi], preferred_element_type=jnp.float32)
        rows = unit[:, lo:hi] * (1.0 + scale[:R]) + shift[:R]
        tail = frames_tail if j == 0 else jnp.zeros((Rp - R, wide), jnp.float32)
        own[j] = jnp.concatenate([rows, tail], axis=0).astype(jnp.bfloat16)
        if j == 0:
            pl.semaphore_wait(barrier, len(greeted))

        @pl.when(k != h)
        def _():
            swap_copy(j).start()

        @pl.when(k == h)
        def _():
            buf[0, j, k] = own[j]

    def slot(way, s):
        if s == 0:
            return 0
        if s == mid:
            return mid
        return s if way == 0 else mid + s

    def ring_copy(way, s, j):
        return remote(
            buf.at[slot(way, s), j, k], buf.at[slot(way, s + 1), j, k],
            ring_send.at[way, s, j], ring_recv.at[way, s, j], right if way == 0 else left,
        )

    def opposite_copy():
        source = jnp.where(p % 2 == 0, slot(0, mid - 1), slot(1, mid - 1))
        return remote(buf.at[source, 1, k], buf.at[mid, 1, k], opp_send, opp_recv, pair_peer)

    def core_copy(sl, j):
        return remote(buf.at[sl, j, k], buf.at[sl, j, k], core_send.at[sl, j], core_recv.at[sl, j], core_peer)

    def core_wait(sl):
        for j in range(CHUNKS):
            remote(
                buf.at[sl, j, 1 - k], buf.at[sl, j, 1 - k], core_send.at[sl, j], core_recv.at[sl, j], core_peer
            ).wait_recv()

    def n_copy(j):
        return remote(local.at[j], plocal.at[j], n_send.at[j], n_recv.at[j], core_peer)

    def first_steps(record):
        for j in range(CHUNKS):
            if not record:
                swap_landed(j).wait_recv()
            for make, what in ((ring_copy, (0, 0, j)), (ring_copy, (1, 0, j)), (core_copy, (0, j))):
                make(*what).start()
                if record:
                    started.append((make, what))

    def pass_on(s, record):
        for j in range(CHUNKS):
            for way in range(2):
                ring_copy(way, s - 1, j).wait_recv()
                sent = [(core_copy, (slot(way, s), j))]
                if s < mid - 1 or (way == 0 and j == 0) or (way == 1 and j == CHUNKS - 1):
                    sent.insert(0, (ring_copy, (way, s, j)))
                if s == mid - 1 and j == 1 and way == 1:
                    sent.insert(0, (opposite_copy, ()))
                for make, what in sent:
                    make(*what).start()
                    if record:
                        started.append((make, what))

    @pl.when(k == h)
    def _():
        first_steps(True)

    for j in range(2):
        local[j] = -gap[:R] * latent_ref[0, :, j * half:(j + 1) * half]
        start(n_copy, j)

    score_scale = HD ** (-0.5) * math.log2(math.e)
    tiles = half // (2 * HD)
    n_rows = 2 * Rp

    def frames_of(sl):
        last = buf[sl, 0, 0, Rp - 16:Rp, :].astype(jnp.float32) + buf[sl, 0, 1, Rp - 16:Rp, :].astype(jnp.float32)
        place = R - (Rp - 16)
        return last[place:place + 1, :n_rows]

    def head_norm(rows):
        return (rows * lax.rsqrt(jnp.mean(rows * rows, axis=-1, keepdims=True) + norm_eps)).astype(jnp.bfloat16)

    def project(sl, i, j):
        cols = pl.ds(pl.multiple_of(j * 2 * HD, 2 * HD), 2 * HD)
        total = None
        for m in range(CHUNKS):
            one = jnp.dot(
                buf[sl, m].reshape(n_rows, wide), wqkv[i, m * wide:(m + 1) * wide, cols],
                preferred_element_type=jnp.float32,
            )
            total = one if total is None else total + one
        return total

    def keys_values(sl, j):
        kk = project(sl, 1, j)
        vv = project(sl, 2, j)
        ones = jnp.ones((n_rows, HD), jnp.bfloat16)
        keys = [head_norm(kk[:, g * HD:(g + 1) * HD]) for g in range(2)]
        values = [
            jnp.concatenate([vv[:, g * HD:(g + 1) * HD].astype(jnp.bfloat16), ones], axis=1) for g in range(2)
        ]
        return keys, values

    def partial_sums(query, key, value, allowed):
        scores = lax.dot_general(query, key, (((1,), (1,)), ((), ())), preferred_element_type=jnp.float32)
        weights = jnp.where(allowed, jnp.exp2(scores * score_scale), 0.0).astype(jnp.bfloat16)
        return jnp.dot(weights, value, preferred_element_type=jnp.float32)

    def attend(sl):
        key_frame = frames_of(sl)

        def tile(j, carry):
            keys, values = keys_values(sl, j)
            allowed = key_frame <= qframe[...].reshape(n_rows, 1)
            for g in range(2):
                part = partial_sums(qbuf[j, g].reshape(n_rows, HD), keys[g], values[g], allowed)
                acc[j, g] += part.reshape(2, Rp, 2 * HD)
            return carry

        lax.fori_loop(0, tiles, tile, 0)

    def project_block(b):
        def tile(j, carry):
            cols = pl.ds(pl.multiple_of(j * 2 * HD, 2 * HD), 2 * HD)
            parts = []
            for i in range(3):
                total = None
                for m in range(CHUNKS):
                    one = jnp.dot(
                        buf[0, m, b], wqkv[i, m * wide:(m + 1) * wide, cols], preferred_element_type=jnp.float32
                    )
                    total = one if total is None else total + one
                parts.append(total)
            ones = jnp.ones((Rp, HD), jnp.bfloat16)
            for g in range(2):
                at = slice(g * HD, (g + 1) * HD)
                qbuf[j, g, b] = head_norm(parts[0][:, at])
                kbuf[j, g, b] = head_norm(parts[1][:, at])
                vbuf[j, g, b] = jnp.concatenate([parts[2][:, at].astype(jnp.bfloat16), ones], axis=1)
            return carry

        lax.fori_loop(0, tiles, tile, 0)

    for i in range(3):
        loads[1 + i].wait()

    @pl.when(k != h)
    def _():
        core_wait(0)

    project_block(h)

    @pl.when(k != h)
    def _():
        first_steps(False)

    for j in range(2):
        gate = jnp.dot(feat, wmod[:, 2 * D + j * half:2 * D + (j + 1) * half], preferred_element_type=jnp.float32)
        negate[j] = -gap * gate

    @pl.when(k == h)
    def _():
        pass_on(1, True)
        core_wait(0)

    project_block(1 - h)
    diagonal = lax.broadcasted_iota(jnp.int32, (n_rows, n_rows), 0) == lax.broadcasted_iota(
        jnp.int32, (n_rows, n_rows), 1
    )
    own_frame = frames_of(0)
    own_query = jnp.sum(jnp.where(diagonal, own_frame, 0.0), axis=1, keepdims=True)
    qframe[...] = own_query.reshape(2, Rp, 1)

    def own_tile(j, carry):
        allowed = own_frame <= qframe[...].reshape(n_rows, 1)
        for g in range(2):
            part = partial_sums(
                qbuf[j, g].reshape(n_rows, HD), kbuf[j, g].reshape(n_rows, HD),
                vbuf[j, g].reshape(n_rows, 2 * HD), allowed,
            )
            acc[j, g] = part.reshape(2, Rp, 2 * HD)
        return carry

    lax.fori_loop(0, tiles, own_tile, 0)

    @pl.when(k != h)
    def _():
        pass_on(1, False)

    def later(d):
        return {"tm": 2 * ((a + d) % pairs) + k}

    def xa_copy(d):
        return remote(xa, xar.at[d - 1], xa_send.at[d - 1], xa_recv.at[d - 1], later(d))

    def ya_copy(d):
        return remote(xar.at[d - 1], yar.at[d - 1], ya_send.at[d - 1], ya_recv.at[d - 1], core_peer)

    first_rows = (Rp // 2 + 15) // 16 * 16
    bands = [(0, first_rows), (first_rows, Rp)]

    def band(ref, i):
        return ref.at[bands[i][0]:bands[i][1]]

    def x_copy(d, i):
        return remote(
            band(xs, i), band(xr.at[d - 1], i), x_send.at[d - 1, i], x_recv.at[d - 1, i], later(d)
        )

    def y_copy(d, i):
        return remote(
            band(xr.at[d - 1], i), band(yr.at[d - 1], i), y_send.at[d - 1, i], y_recv.at[d - 1, i], core_peer
        )

    for j in range(2):
        n_copy(j).wait_recv()
    xa[...] = local[k] + plocal[k]
    for d in range(1, pairs):
        @pl.when(a + d < pairs)
        def _():
            xa_copy(d).start()

    for j in range(2):
        base[j] = jnp.where(k == 1, local[j] + plocal[j], local[j])

    for s in range(1, mid):
        if s > 1:
            pass_on(s, True)
        for way in range(2):
            core_wait(slot(way, s))
            attend(slot(way, s))

    for d in range(1, pairs):
        @pl.when(a >= d)
        def _():
            xa_copy(d).wait_recv()
            ya_copy(d).start()

    ring_copy(0, mid - 1, 0).wait_recv()
    start(core_copy, mid, 0)
    opposite_copy().wait_recv()
    start(core_copy, mid, 1)
    ring_copy(1, mid - 1, CHUNKS - 1).wait_recv()
    start(core_copy, mid, CHUNKS - 1)
    core_wait(mid)

    def last_tile(j, carry):
        keys, values = keys_values(mid, j)
        for g in range(2):
            kbuf[j, g] = keys[g].reshape(2, Rp, HD)
            vbuf[j, g] = values[g].reshape(2, Rp, 2 * HD)
        return carry

    lax.fori_loop(0, tiles, last_tile, 0)
    last_frame = frames_of(mid)

    def finish(b, m, i):
        lo, hi = bands[i]
        allowed = last_frame <= qframe[b, lo:hi]
        for j in range(tiles):
            for g in range(2):
                part = partial_sums(
                    qbuf[j, g, b, lo:hi], kbuf[j, g].reshape(n_rows, HD), vbuf[j, g].reshape(n_rows, 2 * HD), allowed
                )
                full = acc[j, g, b, lo:hi] + part
                first = (2 * j + g) * HD
                atts[m, lo:hi, first:first + HD] = (full[:, :HD] / full[:, HD:]).astype(jnp.bfloat16)

    def away(i):
        return remote(
            band(atts.at[0], i), band(attr.at[k], i), att_send.at[0, i], att_recv.at[k, i],
            {"tm": 2 * a + h, "ctx": (1 - h) * ring + r},
        )

    def across(i):
        return remote(
            band(atts.at[1], i), band(attr.at[k], i), att_send.at[1, i], att_recv.at[k, i], core_peer
        )

    for i in range(2):
        finish(1 - h, 0, i)
        start(away, i)
    for i in range(2):
        finish(h, 1, i)

        @pl.when(k != h)
        def _():
            across(i).start()

    @pl.when(k == h)
    def _():
        attr[k] = atts[1]

    for d in range(1, pairs):
        @pl.when(a >= d)
        def _():
            ya_copy(d).wait_recv()
            base[k] += xar[d - 1]
            base[1 - k] += yar[d - 1]

    loads[4].wait()

    def d_copy(j, i):
        return remote(band(db.at[j], i), band(pdb.at[j], i), d_send.at[j, i], d_recv.at[j, i], core_peer)

    for i in range(2):
        lo, hi = bands[i]
        for m in range(2):
            @pl.when(jnp.logical_not(jnp.logical_and(k == h, k == m)))
            def _():
                remote(
                    band(atts.at[m], i), band(attr.at[m], i), att_send.at[m, i], att_recv.at[m, i],
                    {"tm": 2 * a + m, "ctx": k * ring + r},
                ).wait_recv()

        for j in range(2):
            branch = jnp.zeros((hi - lo, half), jnp.float32)
            for m in range(2):
                branch += jnp.dot(
                    attr[m, lo:hi], wo[m * half:(m + 1) * half, j * half:(j + 1) * half],
                    preferred_element_type=jnp.float32,
                )
            drift[j, lo:hi] = negate[j, lo:hi] * branch
            db[j, lo:hi] = drift[j, lo:hi].astype(jnp.bfloat16)
            start(d_copy, j, i)
        for j in range(2):
            d_copy(j, i).wait_recv()
        xs[lo:hi] = (drift[k, lo:hi] + pdb[k, lo:hi].astype(jnp.float32)).astype(jnp.bfloat16)
        for d in range(1, pairs):
            @pl.when(a + d < pairs)
            def _():
                x_copy(d, i).start()

    for j in range(2):
        here = base[j] + drift[j, :R]
        base[j] = jnp.where(k == 1, here + pdb[j].astype(jnp.float32)[:R], here)

    for d in range(1, pairs):
        @pl.when(a >= d)
        def _():
            for i in range(2):
                x_copy(d, i).wait_recv()
                y_copy(d, i).start()
            base[k] += xr[d - 1].astype(jnp.float32)[:R]
            for i in range(2):
                y_copy(d, i).wait_recv()
            base[1 - k] += yr[d - 1].astype(jnp.float32)[:R]

    for j in range(2):
        out_ref[0, :, j * half:(j + 1) * half] = base[j]

    for make, what in started:
        make(*what).wait_send()

    @pl.when(k != h)
    def _():
        for j in range(CHUNKS):
            swap_copy(j).wait_send()
        for i in range(2):
            across(i).wait_send()

    for d in range(1, pairs):
        @pl.when(a + d < pairs)
        def _():
            xa_copy(d).wait_send()
            for i in range(2):
                x_copy(d, i).wait_send()

        @pl.when(a >= d)
        def _():
            ya_copy(d).wait_send()
            for i in range(2):
                y_copy(d, i).wait_send()


def per_device(tm_size, ctx_size, iterate, anchor, frame_index, noise_steps, qkv_weight, out_weight, mod_weight):
    R, D = anchor.shape
    half = D // 2
    wide = D // CHUNKS
    ring = ctx_size // 2
    pairs = tm_size // 2
    far = max(pairs - 1, 1)
    mid = ring // 2
    Rp = (R + 1 + 15) // 16 * 16
    tiles = half // (2 * HD)
    vmem = pl.BlockSpec(memory_space=pltpu.VMEM)
    hbm = pl.BlockSpec(memory_space=pltpu.HBM)
    dma = pltpu.SemaphoreType.DMA
    f32, bf16 = jnp.float32, jnp.bfloat16
    total = pl.pallas_call(
        functools.partial(kernel, tm_size, ctx_size),
        out_shape=jax.ShapeDtypeStruct((1, R, D), f32),
        in_specs=[vmem, vmem, pl.BlockSpec(memory_space=pltpu.SMEM)] + [hbm] * 3,
        out_specs=vmem,
        scratch_shapes=[
            pltpu.VMEM((3, D, half), bf16),
            pltpu.VMEM((D, D), bf16),
            pltpu.VMEM(mod_weight.shape, bf16),
            pltpu.VMEM((CHUNKS, Rp, wide), bf16),
            pltpu.VMEM((ring, CHUNKS, 2, Rp, wide), bf16),
            pltpu.VMEM((tiles, 2, 2, Rp, HD), bf16),
            pltpu.VMEM((2, Rp, 1), f32),
            pltpu.VMEM((tiles, 2, 2, Rp, 2 * HD), f32),
            pltpu.VMEM((tiles, 2, 2, Rp, HD), bf16),
            pltpu.VMEM((tiles, 2, 2, Rp, 2 * HD), bf16),
            pltpu.VMEM((2, Rp, half), bf16),
            pltpu.VMEM((2, Rp, half), bf16),
            pltpu.VMEM((2, Rp, half), f32),
            pltpu.VMEM((2, R, half), f32),
            pltpu.VMEM((2, R, half), f32),
            pltpu.VMEM((2, R, half), f32),
            pltpu.VMEM((2, Rp, half), f32),
            pltpu.VMEM((2, Rp, half), bf16),
            pltpu.VMEM((2, Rp, half), bf16),
            pltpu.VMEM((R, half), f32),
            pltpu.VMEM((far, R, half), f32),
            pltpu.VMEM((far, R, half), f32),
            pltpu.VMEM((Rp, half), bf16),
            pltpu.VMEM((far, Rp, half), bf16),
            pltpu.VMEM((far, Rp, half), bf16),
            dma((5,)),
            dma((CHUNKS,)), dma((CHUNKS,)),
            dma((2, mid, CHUNKS)), dma((2, mid, CHUNKS)),
            dma, dma,
            dma((ring, CHUNKS)), dma((ring, CHUNKS)),
            dma((2, 2)), dma((2, 2)),
            dma((2,)), dma((2,)),
            dma((2, 2)), dma((2, 2)),
            dma((far,)), dma((far,)),
            dma((far,)), dma((far,)),
            dma((far, 2)), dma((far, 2)),
            dma((far, 2)), dma((far, 2)),
        ],
        compiler_params=pltpu.CompilerParams(
            collective_id=0, has_side_effects=True, vmem_limit_bytes=56 * 1024 * 1024
        ),
    )(iterate, frame_index[None, :], noise_steps, qkv_weight, out_weight, mod_weight)
    return anchor[None] + total


def solution(mesh):
    placed = (P("tm", "ctx", None), P("ctx", None), P("ctx"), P("tm", None), P(), P(), P())
    return jax.shard_map(
        functools.partial(per_device, mesh.shape["tm"], mesh.shape["ctx"]),
        mesh=mesh, in_specs=placed, out_specs=P("tm", "ctx", None), check_vma=False,
    )
```

```python
import functools
import math

import jax
import jax.numpy as jnp
from jax import lax
from jax.experimental import pallas as pl
from jax.experimental.pallas import tpu as pltpu
from jax.sharding import PartitionSpec as P

HD = 128
NSCHED = 12
MESH = pl.DeviceIdType.MESH

shift_factor = 5.0
norm_eps = 1e-06


def noise_level(level_index):
    fraction = level_index / NSCHED
    return shift_factor * fraction / (1.0 + (shift_factor - 1.0) * fraction)


CHUNKS = 3


def kernel(
    tm_size, ctx_size,
    latent_ref, frame_ref, steps_ref, qkv_ref, wo_ref, mod_ref,
    out_ref,
    wqkv, wo, wmod, own, buf, qbuf, qframe, acc, kbuf, vbuf, atts, attr, negate, local, plocal, base, drift,
    db, pdb, xa, xar, yar, xs, xr, yr,
    w_sem, swap_send, swap_recv, ring_send, ring_recv, opp_send, opp_recv, core_send, core_recv,
    att_send, att_recv, n_send, n_recv, d_send, d_recv, xa_send, xa_recv, ya_send, ya_recv,
    x_send, x_recv, y_send, y_recv,
):
    R, D = latent_ref.shape[1], latent_ref.shape[2]
    half = D // 2
    wide = D // CHUNKS
    Rp = own.shape[1]
    ring = ctx_size // 2
    pairs = tm_size // 2
    mid = ring // 2
    t = lax.axis_index("tm")
    c = lax.axis_index("ctx")
    a, k = t // 2, t % 2
    h, r = c // ring, c % ring
    u = r // 2
    p = 2 * u + (r % 2 + u) % 2

    def at_ring(q):
        v = q // 2
        return h * ring + 2 * v + (q % 2 + v) % 2

    core_peer = {"tm": 2 * a + 1 - k}
    swap_peer = {"tm": 2 * a + h, "ctx": k * ring + r}
    right = {"ctx": at_ring((p + 1) % ring)}
    left = {"ctx": at_ring((p + ring - 1) % ring)}
    pair_peer = {"ctx": at_ring(p + 1 - 2 * (p % 2))}

    loads = [pltpu.make_async_copy(mod_ref, wmod, w_sem.at[0])]
    for i in range(3):
        col = pl.multiple_of(i * D + k * half, 128)
        loads.append(pltpu.make_async_copy(qkv_ref.at[:, pl.ds(col, half)], wqkv.at[i], w_sem.at[1 + i]))
    loads.append(pltpu.make_async_copy(wo_ref, wo, w_sem.at[4]))
    loads[0].start()

    barrier = pltpu.get_barrier_semaphore()
    greeted = [
        core_peer,
        {"tm": 2 * a + k, "ctx": (1 - h) * ring + r},
        {"tm": 2 * a + 1 - k, "ctx": (1 - h) * ring + r},
        left,
        right,
    ]
    for d in range(1, pairs):
        greeted.append({"tm": 2 * ((a + d) % pairs) + k})
    for peer in greeted:
        pl.semaphore_signal(barrier, inc=1, device_id=peer, device_id_type=MESH)

    def remote(src, dst, s_sem, r_sem, peer):
        return pltpu.make_async_remote_copy(
            src_ref=src, dst_ref=dst, send_sem=s_sem, recv_sem=r_sem, device_id=peer, device_id_type=MESH
        )

    started = []

    def start(make, *what):
        make(*what).start()
        started.append((make, what))

    def swap_copy(j):
        return remote(own.at[j], buf.at[0, j, h], swap_send.at[j], swap_recv.at[j], swap_peer)

    def swap_landed(j):
        return remote(own.at[j], buf.at[0, j, k], swap_send.at[j], swap_recv.at[j], swap_peer)

    x = latent_ref[0]
    center = x - jnp.mean(x, axis=-1, keepdims=True)
    spread = jnp.mean(center * center, axis=-1, keepdims=True)
    unit = center * lax.rsqrt(spread + norm_eps)

    row_place = lax.broadcasted_iota(jnp.int32, (Rp, R), 0)
    lane_place = lax.broadcasted_iota(jnp.int32, (Rp, R), 1)
    frame_row = frame_ref[...].astype(jnp.float32)
    frame_col = jnp.sum(jnp.where(row_place == lane_place, frame_row, 0.0), axis=1, keepdims=True)
    level_index = jnp.zeros((Rp, 1), jnp.float32)
    for f in range(steps_ref.shape[1]):
        level_index += jnp.where(frame_col == float(f), steps_ref[0, f].astype(jnp.float32), 0.0)
    upper = noise_level(level_index + 1.0)
    gap = upper - noise_level(level_index)
    half_freq = mod_ref.shape[0] // 2
    rate_place = lax.broadcasted_iota(jnp.int32, (1, half_freq), 1).astype(jnp.float32)
    rates = jnp.exp(-math.log(10000.0) * rate_place / half_freq)
    angles = (1000.0 * upper) * rates
    feat = jnp.concatenate([jnp.cos(angles), jnp.sin(angles)], axis=1).astype(jnp.bfloat16)
    here_row = lax.broadcasted_iota(jnp.int32, (Rp, wide), 0)
    here_lane = lax.broadcasted_iota(jnp.int32, (Rp, wide), 1)
    never = float(4 * steps_ref.shape[1])
    told = jnp.where(here_row < R, frame_col, never)
    frames_out = jnp.sum(jnp.where(here_lane == here_row + h * Rp, told, 0.0), axis=0, keepdims=True)
    spare_row = lax.broadcasted_iota(jnp.int32, (Rp - R, wide), 0)
    frames_tail = jnp.where(spare_row == 0, frames_out, 0.0)

    loads[0].wait()
    for load in loads[1:]:
        load.start()
    for j in range(CHUNKS):
        lo, hi = j * wide, (j + 1) * wide
        shift = jnp.dot(feat, wmod[:, lo:hi], preferred_element_type=jnp.float32)
        scale = jnp.dot(feat, wmod[:, D + lo:D + hi], preferred_element_type=jnp.float32)
        rows = unit[:, lo:hi] * (1.0 + scale[:R]) + shift[:R]
        tail = frames_tail if j == 0 else jnp.zeros((Rp - R, wide), jnp.float32)
        own[j] = jnp.concatenate([rows, tail], axis=0).astype(jnp.bfloat16)
        if j == 0:
            pl.semaphore_wait(barrier, len(greeted))

        if j == 0:
            @pl.when(k != h)
            def _():
                swap_copy(0).start()

        @pl.when(k == h)
        def _():
            buf[0, j, k] = own[j]

    def slot(way, s):
        if s == 0:
            return 0
        if s == mid:
            return mid
        return s if way == 0 else mid + s

    def ring_copy(way, s, j):
        return remote(
            buf.at[slot(way, s), j, k], buf.at[slot(way, s + 1), j, k],
            ring_send.at[way, s, j], ring_recv.at[way, s, j], right if way == 0 else left,
        )

    def opposite_copy():
        source = jnp.where(p % 2 == 0, slot(0, mid - 1), slot(1, mid - 1))
        return remote(buf.at[source, 1, k], buf.at[mid, 1, k], opp_send, opp_recv, pair_peer)

    def core_copy(sl, j):
        return remote(buf.at[sl, j, k], buf.at[sl, j, k], core_send.at[sl, j], core_recv.at[sl, j], core_peer)

    def core_wait(sl):
        for j in range(CHUNKS):
            remote(
                buf.at[sl, j, 1 - k], buf.at[sl, j, 1 - k], core_send.at[sl, j], core_recv.at[sl, j], core_peer
            ).wait_recv()

    def n_copy(j):
        return remote(local.at[j], plocal.at[j], n_send.at[j], n_recv.at[j], core_peer)

    def ring_step(j, record):
        for way in range(2):
            ring_copy(way, 0, j).start()
            if record:
                started.append((ring_copy, (way, 0, j)))

    def swapped_steps():
        for j in range(CHUNKS):
            if j + 1 < CHUNKS:
                swap_copy(j).wait_send()
                swap_copy(j + 1).start()
            swap_landed(j).wait_recv()
            ring_step(j, False)
            core_copy(0, j).start()

    def pass_on(s, record):
        for j in range(CHUNKS):
            for way in range(2):
                ring_copy(way, s - 1, j).wait_recv()
                sent = [(core_copy, (slot(way, s), j))]
                if s < mid - 1 or (way == 0 and j == 0) or (way == 1 and j == CHUNKS - 1):
                    sent.insert(0, (ring_copy, (way, s, j)))
                if s == mid - 1 and j == 1 and way == 1:
                    sent.insert(0, (opposite_copy, ()))
                for make, what in sent:
                    make(*what).start()
                    if record:
                        started.append((make, what))

    @pl.when(k == h)
    def _():
        ring_step(0, True)
        for j in range(CHUNKS):
            core_copy(0, j).start()
            started.append((core_copy, (0, j)))

    for j in range(2):
        local[j] = -gap[:R] * latent_ref[0, :, j * half:(j + 1) * half]
        start(n_copy, j)

    score_scale = HD ** (-0.5) * math.log2(math.e)
    tiles = half // (2 * HD)
    n_rows = 2 * Rp

    def frames_of(sl):
        last = buf[sl, 0, 0, Rp - 16:Rp, :].astype(jnp.float32) + buf[sl, 0, 1, Rp - 16:Rp, :].astype(jnp.float32)
        place = R - (Rp - 16)
        return last[place:place + 1, :n_rows]

    def head_norm(rows):
        return (rows * lax.rsqrt(jnp.mean(rows * rows, axis=-1, keepdims=True) + norm_eps)).astype(jnp.bfloat16)

    def project(sl, i, j):
        cols = pl.ds(pl.multiple_of(j * 2 * HD, 2 * HD), 2 * HD)
        total = None
        for m in range(CHUNKS):
            one = jnp.dot(
                buf[sl, m].reshape(n_rows, wide), wqkv[i, m * wide:(m + 1) * wide, cols],
                preferred_element_type=jnp.float32,
            )
            total = one if total is None else total + one
        return total

    def keys_values(sl, j):
        kk = project(sl, 1, j)
        vv = project(sl, 2, j)
        ones = jnp.ones((n_rows, HD), jnp.bfloat16)
        keys = [head_norm(kk[:, g * HD:(g + 1) * HD]) for g in range(2)]
        values = [
            jnp.concatenate([vv[:, g * HD:(g + 1) * HD].astype(jnp.bfloat16), ones], axis=1) for g in range(2)
        ]
        return keys, values

    def partial_sums(query, key, value, allowed):
        scores = lax.dot_general(query, key, (((1,), (1,)), ((), ())), preferred_element_type=jnp.float32)
        weights = jnp.where(allowed, jnp.exp2(scores * score_scale), 0.0).astype(jnp.bfloat16)
        return jnp.dot(weights, value, preferred_element_type=jnp.float32)

    def attend(sl):
        key_frame = frames_of(sl)

        def tile(j, carry):
            keys, values = keys_values(sl, j)
            allowed = key_frame <= qframe[...].reshape(n_rows, 1)
            for g in range(2):
                part = partial_sums(qbuf[j, g].reshape(n_rows, HD), keys[g], values[g], allowed)
                acc[j, g] += part.reshape(2, Rp, 2 * HD)
            return carry

        lax.fori_loop(0, tiles, tile, 0)

    def project_block(b):
        def tile(j, carry):
            cols = pl.ds(pl.multiple_of(j * 2 * HD, 2 * HD), 2 * HD)
            parts = []
            for i in range(3):
                total = None
                for m in range(CHUNKS):
                    one = jnp.dot(
                        buf[0, m, b], wqkv[i, m * wide:(m + 1) * wide, cols], preferred_element_type=jnp.float32
                    )
                    total = one if total is None else total + one
                parts.append(total)
            ones = jnp.ones((Rp, HD), jnp.bfloat16)
            for g in range(2):
                at = slice(g * HD, (g + 1) * HD)
                qbuf[j, g, b] = head_norm(parts[0][:, at])
                kbuf[j, g, b] = head_norm(parts[1][:, at])
                vbuf[j, g, b] = jnp.concatenate([parts[2][:, at].astype(jnp.bfloat16), ones], axis=1)
            return carry

        lax.fori_loop(0, tiles, tile, 0)

    for i in range(3):
        loads[1 + i].wait()

    @pl.when(k != h)
    def _():
        swapped_steps()
        core_wait(0)

    project_block(h)

    @pl.when(k == h)
    def _():
        for j in range(1, CHUNKS):
            ring_step(j, True)

    for j in range(2):
        gate = jnp.dot(feat, wmod[:, 2 * D + j * half:2 * D + (j + 1) * half], preferred_element_type=jnp.float32)
        negate[j] = -gap * gate

    @pl.when(k == h)
    def _():
        pass_on(1, True)
        core_wait(0)

    project_block(1 - h)
    diagonal = lax.broadcasted_iota(jnp.int32, (n_rows, n_rows), 0) == lax.broadcasted_iota(
        jnp.int32, (n_rows, n_rows), 1
    )
    own_frame = frames_of(0)
    own_query = jnp.sum(jnp.where(diagonal, own_frame, 0.0), axis=1, keepdims=True)
    qframe[...] = own_query.reshape(2, Rp, 1)

    def own_tile(j, carry):
        allowed = own_frame <= qframe[...].reshape(n_rows, 1)
        for g in range(2):
            part = partial_sums(
                qbuf[j, g].reshape(n_rows, HD), kbuf[j, g].reshape(n_rows, HD),
                vbuf[j, g].reshape(n_rows, 2 * HD), allowed,
            )
            acc[j, g] = part.reshape(2, Rp, 2 * HD)
        return carry

    lax.fori_loop(0, tiles, own_tile, 0)

    @pl.when(k != h)
    def _():
        pass_on(1, False)

    def later(d):
        return {"tm": 2 * ((a + d) % pairs) + k}

    def xa_copy(d):
        return remote(xa, xar.at[d - 1], xa_send.at[d - 1], xa_recv.at[d - 1], later(d))

    def ya_copy(d):
        return remote(xar.at[d - 1], yar.at[d - 1], ya_send.at[d - 1], ya_recv.at[d - 1], core_peer)

    first_rows = (Rp // 2 + 15) // 16 * 16
    bands = [(0, first_rows), (first_rows, Rp)]

    def band(ref, i):
        return ref.at[bands[i][0]:bands[i][1]]

    def x_copy(d, i):
        return remote(
            band(xs, i), band(xr.at[d - 1], i), x_send.at[d - 1, i], x_recv.at[d - 1, i], later(d)
        )

    def y_copy(d, i):
        return remote(
            band(xr.at[d - 1], i), band(yr.at[d - 1], i), y_send.at[d - 1, i], y_recv.at[d - 1, i], core_peer
        )

    for j in range(2):
        n_copy(j).wait_recv()
    xa[...] = local[k] + plocal[k]
    for d in range(1, pairs):
        @pl.when(a + d < pairs)
        def _():
            xa_copy(d).start()

    for j in range(2):
        base[j] = jnp.where(k == 1, local[j] + plocal[j], local[j])

    for s in range(1, mid):
        if s > 1:
            pass_on(s, True)
        for way in range(2):
            core_wait(slot(way, s))
            attend(slot(way, s))

    for d in range(1, pairs):
        @pl.when(a >= d)
        def _():
            xa_copy(d).wait_recv()
            ya_copy(d).start()

    ring_copy(0, mid - 1, 0).wait_recv()
    start(core_copy, mid, 0)
    opposite_copy().wait_recv()
    start(core_copy, mid, 1)
    ring_copy(1, mid - 1, CHUNKS - 1).wait_recv()
    start(core_copy, mid, CHUNKS - 1)
    core_wait(mid)

    def last_tile(j, carry):
        keys, values = keys_values(mid, j)
        for g in range(2):
            kbuf[j, g] = keys[g].reshape(2, Rp, HD)
            vbuf[j, g] = values[g].reshape(2, Rp, 2 * HD)
        return carry

    lax.fori_loop(0, tiles, last_tile, 0)
    last_frame = frames_of(mid)

    def finish(b, m, i):
        lo, hi = bands[i]
        allowed = last_frame <= qframe[b, lo:hi]
        for j in range(tiles):
            for g in range(2):
                part = partial_sums(
                    qbuf[j, g, b, lo:hi], kbuf[j, g].reshape(n_rows, HD), vbuf[j, g].reshape(n_rows, 2 * HD), allowed
                )
                full = acc[j, g, b, lo:hi] + part
                first = (2 * j + g) * HD
                atts[m, lo:hi, first:first + HD] = (full[:, :HD] / full[:, HD:]).astype(jnp.bfloat16)

    def away(i):
        return remote(
            band(atts.at[0], i), band(attr.at[k], i), att_send.at[0, i], att_recv.at[k, i],
            {"tm": 2 * a + h, "ctx": (1 - h) * ring + r},
        )

    def across(i):
        return remote(
            band(atts.at[1], i), band(attr.at[k], i), att_send.at[1, i], att_recv.at[k, i], core_peer
        )

    for i in range(2):
        finish(1 - h, 0, i)
        if i == 0:
            away(0).start()
    for i in range(2):
        finish(h, 1, i)

        @pl.when(k != h)
        def _():
            across(i).start()

    away(0).wait_send()
    start(away, 1)

    @pl.when(k == h)
    def _():
        attr[k] = atts[1]

    for d in range(1, pairs):
        @pl.when(a >= d)
        def _():
            ya_copy(d).wait_recv()
            base[k] += xar[d - 1]
            base[1 - k] += yar[d - 1]

    loads[4].wait()

    def d_copy(j, i):
        return remote(band(db.at[j], i), band(pdb.at[j], i), d_send.at[j, i], d_recv.at[j, i], core_peer)

    for i in range(2):
        lo, hi = bands[i]
        for m in range(2):
            @pl.when(jnp.logical_not(jnp.logical_and(k == h, k == m)))
            def _():
                remote(
                    band(atts.at[m], i), band(attr.at[m], i), att_send.at[m, i], att_recv.at[m, i],
                    {"tm": 2 * a + m, "ctx": k * ring + r},
                ).wait_recv()

        for j in range(2):
            branch = jnp.zeros((hi - lo, half), jnp.float32)
            for m in range(2):
                branch += jnp.dot(
                    attr[m, lo:hi], wo[m * half:(m + 1) * half, j * half:(j + 1) * half],
                    preferred_element_type=jnp.float32,
                )
            drift[j, lo:hi] = negate[j, lo:hi] * branch
            db[j, lo:hi] = drift[j, lo:hi].astype(jnp.bfloat16)
            start(d_copy, j, i)
        for j in range(2):
            d_copy(j, i).wait_recv()
        xs[lo:hi] = (drift[k, lo:hi] + pdb[k, lo:hi].astype(jnp.float32)).astype(jnp.bfloat16)
        for d in range(1, pairs):
            @pl.when(a + d < pairs)
            def _():
                x_copy(d, i).start()

    for j in range(2):
        here = base[j] + drift[j, :R]
        base[j] = jnp.where(k == 1, here + pdb[j].astype(jnp.float32)[:R], here)

    for d in range(1, pairs):
        @pl.when(a >= d)
        def _():
            for i in range(2):
                x_copy(d, i).wait_recv()
                y_copy(d, i).start()
            base[k] += xr[d - 1].astype(jnp.float32)[:R]
            for i in range(2):
                y_copy(d, i).wait_recv()
            base[1 - k] += yr[d - 1].astype(jnp.float32)[:R]

    for j in range(2):
        out_ref[0, :, j * half:(j + 1) * half] = base[j]

    for make, what in started:
        make(*what).wait_send()

    @pl.when(k != h)
    def _():
        swap_copy(CHUNKS - 1).wait_send()
        for i in range(2):
            across(i).wait_send()

    for d in range(1, pairs):
        @pl.when(a + d < pairs)
        def _():
            xa_copy(d).wait_send()
            for i in range(2):
                x_copy(d, i).wait_send()

        @pl.when(a >= d)
        def _():
            ya_copy(d).wait_send()
            for i in range(2):
                y_copy(d, i).wait_send()


def per_device(tm_size, ctx_size, iterate, anchor, frame_index, noise_steps, qkv_weight, out_weight, mod_weight):
    R, D = anchor.shape
    half = D // 2
    wide = D // CHUNKS
    ring = ctx_size // 2
    pairs = tm_size // 2
    far = max(pairs - 1, 1)
    mid = ring // 2
    Rp = (R + 1 + 15) // 16 * 16
    tiles = half // (2 * HD)
    vmem = pl.BlockSpec(memory_space=pltpu.VMEM)
    hbm = pl.BlockSpec(memory_space=pltpu.HBM)
    dma = pltpu.SemaphoreType.DMA
    f32, bf16 = jnp.float32, jnp.bfloat16
    total = pl.pallas_call(
        functools.partial(kernel, tm_size, ctx_size),
        out_shape=jax.ShapeDtypeStruct((1, R, D), f32),
        in_specs=[vmem, vmem, pl.BlockSpec(memory_space=pltpu.SMEM)] + [hbm] * 3,
        out_specs=vmem,
        scratch_shapes=[
            pltpu.VMEM((3, D, half), bf16),
            pltpu.VMEM((D, D), bf16),
            pltpu.VMEM(mod_weight.shape, bf16),
            pltpu.VMEM((CHUNKS, Rp, wide), bf16),
            pltpu.VMEM((ring, CHUNKS, 2, Rp, wide), bf16),
            pltpu.VMEM((tiles, 2, 2, Rp, HD), bf16),
            pltpu.VMEM((2, Rp, 1), f32),
            pltpu.VMEM((tiles, 2, 2, Rp, 2 * HD), f32),
            pltpu.VMEM((tiles, 2, 2, Rp, HD), bf16),
            pltpu.VMEM((tiles, 2, 2, Rp, 2 * HD), bf16),
            pltpu.VMEM((2, Rp, half), bf16),
            pltpu.VMEM((2, Rp, half), bf16),
            pltpu.VMEM((2, Rp, half), f32),
            pltpu.VMEM((2, R, half), f32),
            pltpu.VMEM((2, R, half), f32),
            pltpu.VMEM((2, R, half), f32),
            pltpu.VMEM((2, Rp, half), f32),
            pltpu.VMEM((2, Rp, half), bf16),
            pltpu.VMEM((2, Rp, half), bf16),
            pltpu.VMEM((R, half), f32),
            pltpu.VMEM((far, R, half), f32),
            pltpu.VMEM((far, R, half), f32),
            pltpu.VMEM((Rp, half), bf16),
            pltpu.VMEM((far, Rp, half), bf16),
            pltpu.VMEM((far, Rp, half), bf16),
            dma((5,)),
            dma((CHUNKS,)), dma((CHUNKS,)),
            dma((2, mid, CHUNKS)), dma((2, mid, CHUNKS)),
            dma, dma,
            dma((ring, CHUNKS)), dma((ring, CHUNKS)),
            dma((2, 2)), dma((2, 2)),
            dma((2,)), dma((2,)),
            dma((2, 2)), dma((2, 2)),
            dma((far,)), dma((far,)),
            dma((far,)), dma((far,)),
            dma((far, 2)), dma((far, 2)),
            dma((far, 2)), dma((far, 2)),
        ],
        compiler_params=pltpu.CompilerParams(
            collective_id=0, has_side_effects=True, vmem_limit_bytes=56 * 1024 * 1024
        ),
    )(iterate, frame_index[None, :], noise_steps, qkv_weight, out_weight, mod_weight)
    return anchor[None] + total


def solution(mesh):
    placed = (P("tm", "ctx", None), P("ctx", None), P("ctx"), P("tm", None), P(), P(), P())
    return jax.shard_map(
        functools.partial(per_device, mesh.shape["tm"], mesh.shape["ctx"]),
        mesh=mesh, in_specs=placed, out_specs=P("tm", "ctx", None), check_vma=False,
    )
```

```python
import functools
import math

import jax
import jax.numpy as jnp
from jax import lax
from jax.experimental import pallas as pl
from jax.experimental.pallas import tpu as pltpu
from jax.sharding import PartitionSpec as P

HD = 128
NSCHED = 12
MESH = pl.DeviceIdType.MESH

shift_factor = 5.0
norm_eps = 1e-06


def noise_level(level_index):
    fraction = level_index / NSCHED
    return shift_factor * fraction / (1.0 + (shift_factor - 1.0) * fraction)


CHUNKS = 3


def kernel(
    tm_size, ctx_size,
    latent_ref, frame_ref, steps_ref, qkv_ref, wo_ref, mod_ref,
    out_ref,
    wqkv, wo, wmod, own, buf, qbuf, qframe, acc, kbuf, vbuf, atts, attr, negate, local, plocal, base, drift,
    db, pdb, xa, xar, yar, xs, xr, yr,
    w_sem, swap_send, swap_recv, ring_send, ring_recv, opp_send, opp_recv, core_send, core_recv,
    att_send, att_recv, n_send, n_recv, d_send, d_recv, xa_send, xa_recv, ya_send, ya_recv,
    x_send, x_recv, y_send, y_recv,
):
    R, D = latent_ref.shape[1], latent_ref.shape[2]
    half = D // 2
    wide = D // CHUNKS
    Rp = own.shape[1]
    ring = ctx_size // 2
    pairs = tm_size // 2
    mid = ring // 2
    t = lax.axis_index("tm")
    c = lax.axis_index("ctx")
    a, k = t // 2, t % 2
    h, r = c // ring, c % ring
    u = r // 2
    p = 2 * u + (r % 2 + u) % 2

    def at_ring(q):
        v = q // 2
        return h * ring + 2 * v + (q % 2 + v) % 2

    core_peer = {"tm": 2 * a + 1 - k}
    swap_peer = {"tm": 2 * a + h, "ctx": k * ring + r}
    right = {"ctx": at_ring((p + 1) % ring)}
    left = {"ctx": at_ring((p + ring - 1) % ring)}
    pair_peer = {"ctx": at_ring(p + 1 - 2 * (p % 2))}

    loads = [pltpu.make_async_copy(mod_ref, wmod, w_sem.at[0])]
    for i in range(3):
        col = pl.multiple_of(i * D + k * half, 128)
        loads.append(pltpu.make_async_copy(qkv_ref.at[:, pl.ds(col, half)], wqkv.at[i], w_sem.at[1 + i]))
    loads.append(pltpu.make_async_copy(wo_ref, wo, w_sem.at[4]))
    loads[0].start()

    barrier = pltpu.get_barrier_semaphore()
    greeted = [
        core_peer,
        {"tm": 2 * a + k, "ctx": (1 - h) * ring + r},
        {"tm": 2 * a + 1 - k, "ctx": (1 - h) * ring + r},
        left,
        right,
    ]
    for d in range(1, pairs):
        greeted.append({"tm": 2 * ((a + d) % pairs) + k})
    for peer in greeted:
        pl.semaphore_signal(barrier, inc=1, device_id=peer, device_id_type=MESH)

    def remote(src, dst, s_sem, r_sem, peer):
        return pltpu.make_async_remote_copy(
            src_ref=src, dst_ref=dst, send_sem=s_sem, recv_sem=r_sem, device_id=peer, device_id_type=MESH
        )

    started = []

    def start(make, *what):
        make(*what).start()
        started.append((make, what))

    def swap_copy(j):
        return remote(own.at[j], buf.at[0, j, h], swap_send.at[j], swap_recv.at[j], swap_peer)

    def swap_landed(j):
        return remote(own.at[j], buf.at[0, j, k], swap_send.at[j], swap_recv.at[j], swap_peer)

    x = latent_ref[0]
    center = x - jnp.mean(x, axis=-1, keepdims=True)
    spread = jnp.mean(center * center, axis=-1, keepdims=True)
    unit = center * lax.rsqrt(spread + norm_eps)

    row_place = lax.broadcasted_iota(jnp.int32, (Rp, R), 0)
    lane_place = lax.broadcasted_iota(jnp.int32, (Rp, R), 1)
    frame_row = frame_ref[...].astype(jnp.float32)
    frame_col = jnp.sum(jnp.where(row_place == lane_place, frame_row, 0.0), axis=1, keepdims=True)
    level_index = jnp.zeros((Rp, 1), jnp.float32)
    for f in range(steps_ref.shape[1]):
        level_index += jnp.where(frame_col == float(f), steps_ref[0, f].astype(jnp.float32), 0.0)
    upper = noise_level(level_index + 1.0)
    gap = upper - noise_level(level_index)
    half_freq = mod_ref.shape[0] // 2
    rate_place = lax.broadcasted_iota(jnp.int32, (1, half_freq), 1).astype(jnp.float32)
    rates = jnp.exp(-math.log(10000.0) * rate_place / half_freq)
    angles = (1000.0 * upper) * rates
    feat = jnp.concatenate([jnp.cos(angles), jnp.sin(angles)], axis=1).astype(jnp.bfloat16)
    here_row = lax.broadcasted_iota(jnp.int32, (Rp, wide), 0)
    here_lane = lax.broadcasted_iota(jnp.int32, (Rp, wide), 1)
    never = float(4 * steps_ref.shape[1])
    told = jnp.where(here_row < R, frame_col, never)
    frames_out = jnp.sum(jnp.where(here_lane == here_row + h * Rp, told, 0.0), axis=0, keepdims=True)
    spare_row = lax.broadcasted_iota(jnp.int32, (Rp - R, wide), 0)
    frames_tail = jnp.where(spare_row == 0, frames_out, 0.0)

    loads[0].wait()
    for load in loads[1:]:
        load.start()
    for j in range(CHUNKS):
        lo, hi = j * wide, (j + 1) * wide
        shift = jnp.dot(feat, wmod[:, lo:hi], preferred_element_type=jnp.float32)
        scale = jnp.dot(feat, wmod[:, D + lo:D + hi], preferred_element_type=jnp.float32)
        rows = unit[:, lo:hi] * (1.0 + scale[:R]) + shift[:R]
        tail = frames_tail if j == 0 else jnp.zeros((Rp - R, wide), jnp.float32)
        own[j] = jnp.concatenate([rows, tail], axis=0).astype(jnp.bfloat16)
        if j == 0:
            pl.semaphore_wait(barrier, len(greeted))

        @pl.when(k != h)
        def _():
            swap_copy(j).start()

        @pl.when(k == h)
        def _():
            buf[0, j, k] = own[j]

    def slot(way, s):
        if s == 0:
            return 0
        if s == mid:
            return mid
        return s if way == 0 else mid + s

    def ring_copy(way, s, j):
        return remote(
            buf.at[slot(way, s), j, k], buf.at[slot(way, s + 1), j, k],
            ring_send.at[way, s, j], ring_recv.at[way, s, j], right if way == 0 else left,
        )

    def opposite_copy():
        source = jnp.where(p % 2 == 0, slot(0, mid - 1), slot(1, mid - 1))
        return remote(buf.at[source, 1, k], buf.at[mid, 1, k], opp_send, opp_recv, pair_peer)

    def core_copy(sl, j):
        return remote(buf.at[sl, j, k], buf.at[sl, j, k], core_send.at[sl, j], core_recv.at[sl, j], core_peer)

    def core_wait(sl):
        for j in range(CHUNKS):
            remote(
                buf.at[sl, j, 1 - k], buf.at[sl, j, 1 - k], core_send.at[sl, j], core_recv.at[sl, j], core_peer
            ).wait_recv()

    def n_copy(j):
        return remote(local.at[j], plocal.at[j], n_send.at[j], n_recv.at[j], core_peer)

    def first_steps(record):
        for j in range(CHUNKS):
            if not record:
                swap_landed(j).wait_recv()
            for make, what in ((ring_copy, (0, 0, j)), (ring_copy, (1, 0, j)), (core_copy, (0, j))):
                make(*what).start()
                if record:
                    started.append((make, what))

    def pass_on(s, record):
        for j in range(CHUNKS):
            for way in range(2):
                ring_copy(way, s - 1, j).wait_recv()
                sent = [(core_copy, (slot(way, s), j))]
                if s < mid - 1 or (way == 0 and j == 0) or (way == 1 and j == CHUNKS - 1):
                    sent.insert(0, (ring_copy, (way, s, j)))
                if s == mid - 1 and j == 1 and way == 1:
                    sent.insert(0, (opposite_copy, ()))
                for make, what in sent:
                    make(*what).start()
                    if record:
                        started.append((make, what))

    @pl.when(k == h)
    def _():
        first_steps(True)

    for j in range(2):
        local[j] = -gap[:R] * latent_ref[0, :, j * half:(j + 1) * half]
        start(n_copy, j)

    score_scale = HD ** (-0.5) * math.log2(math.e)
    tiles = half // (2 * HD)
    n_rows = 2 * Rp

    def frames_of(sl):
        last = buf[sl, 0, 0, Rp - 16:Rp, :].astype(jnp.float32) + buf[sl, 0, 1, Rp - 16:Rp, :].astype(jnp.float32)
        place = R - (Rp - 16)
        return last[place:place + 1, :n_rows]

    def head_norm(rows):
        return (rows * lax.rsqrt(jnp.mean(rows * rows, axis=-1, keepdims=True) + norm_eps)).astype(jnp.bfloat16)

    def project(sl, i, j):
        cols = pl.ds(pl.multiple_of(j * 2 * HD, 2 * HD), 2 * HD)
        total = None
        for m in range(CHUNKS):
            one = jnp.dot(
                buf[sl, m].reshape(n_rows, wide), wqkv[i, m * wide:(m + 1) * wide, cols],
                preferred_element_type=jnp.float32,
            )
            total = one if total is None else total + one
        return total

    def keys_values(sl, j):
        kk = project(sl, 1, j)
        vv = project(sl, 2, j)
        ones = jnp.ones((n_rows, HD), jnp.bfloat16)
        keys = [head_norm(kk[:, g * HD:(g + 1) * HD]) for g in range(2)]
        values = [
            jnp.concatenate([vv[:, g * HD:(g + 1) * HD].astype(jnp.bfloat16), ones], axis=1) for g in range(2)
        ]
        return keys, values

    def partial_sums(query, key, value, allowed):
        scores = lax.dot_general(query, key, (((1,), (1,)), ((), ())), preferred_element_type=jnp.float32)
        weights = jnp.where(allowed, jnp.exp2(scores * score_scale), 0.0).astype(jnp.bfloat16)
        return jnp.dot(weights, value, preferred_element_type=jnp.float32)

    def attend(sl):
        key_frame = frames_of(sl)

        def tile(j, carry):
            keys, values = keys_values(sl, j)
            allowed = key_frame <= qframe[...].reshape(n_rows, 1)
            for g in range(2):
                part = partial_sums(qbuf[j, g].reshape(n_rows, HD), keys[g], values[g], allowed)
                acc[j, g] += part.reshape(2, Rp, 2 * HD)
            return carry

        lax.fori_loop(0, tiles, tile, 0)

    def project_block(b):
        def tile(j, carry):
            cols = pl.ds(pl.multiple_of(j * 2 * HD, 2 * HD), 2 * HD)
            parts = []
            for i in range(3):
                total = None
                for m in range(CHUNKS):
                    one = jnp.dot(
                        buf[0, m, b], wqkv[i, m * wide:(m + 1) * wide, cols], preferred_element_type=jnp.float32
                    )
                    total = one if total is None else total + one
                parts.append(total)
            ones = jnp.ones((Rp, HD), jnp.bfloat16)
            for g in range(2):
                at = slice(g * HD, (g + 1) * HD)
                qbuf[j, g, b] = head_norm(parts[0][:, at])
                kbuf[j, g, b] = head_norm(parts[1][:, at])
                vbuf[j, g, b] = jnp.concatenate([parts[2][:, at].astype(jnp.bfloat16), ones], axis=1)
            return carry

        lax.fori_loop(0, tiles, tile, 0)

    for i in range(3):
        loads[1 + i].wait()

    @pl.when(k != h)
    def _():
        first_steps(False)
        core_wait(0)

    project_block(h)

    for j in range(2):
        gate = jnp.dot(feat, wmod[:, 2 * D + j * half:2 * D + (j + 1) * half], preferred_element_type=jnp.float32)
        negate[j] = -gap * gate

    @pl.when(k == h)
    def _():
        pass_on(1, True)
        core_wait(0)

    project_block(1 - h)
    diagonal = lax.broadcasted_iota(jnp.int32, (n_rows, n_rows), 0) == lax.broadcasted_iota(
        jnp.int32, (n_rows, n_rows), 1
    )
    own_frame = frames_of(0)
    own_query = jnp.sum(jnp.where(diagonal, own_frame, 0.0), axis=1, keepdims=True)
    qframe[...] = own_query.reshape(2, Rp, 1)

    def own_tile(j, carry):
        allowed = own_frame <= qframe[...].reshape(n_rows, 1)
        for g in range(2):
            part = partial_sums(
                qbuf[j, g].reshape(n_rows, HD), kbuf[j, g].reshape(n_rows, HD),
                vbuf[j, g].reshape(n_rows, 2 * HD), allowed,
            )
            acc[j, g] = part.reshape(2, Rp, 2 * HD)
        return carry

    lax.fori_loop(0, tiles, own_tile, 0)

    @pl.when(k != h)
    def _():
        pass_on(1, False)

    def later(d):
        return {"tm": 2 * ((a + d) % pairs) + k}

    def xa_copy(d):
        return remote(xa, xar.at[d - 1], xa_send.at[d - 1], xa_recv.at[d - 1], later(d))

    def ya_copy(d):
        return remote(xar.at[d - 1], yar.at[d - 1], ya_send.at[d - 1], ya_recv.at[d - 1], core_peer)

    first_rows = (Rp // 2 + 15) // 16 * 16
    bands = [(0, first_rows), (first_rows, Rp)]

    def band(ref, i):
        return ref.at[bands[i][0]:bands[i][1]]

    def x_copy(d, i):
        return remote(
            band(xs, i), band(xr.at[d - 1], i), x_send.at[d - 1, i], x_recv.at[d - 1, i], later(d)
        )

    def y_copy(d, i):
        return remote(
            band(xr.at[d - 1], i), band(yr.at[d - 1], i), y_send.at[d - 1, i], y_recv.at[d - 1, i], core_peer
        )

    for j in range(2):
        n_copy(j).wait_recv()
    xa[...] = local[k] + plocal[k]
    for d in range(1, pairs):
        @pl.when(a + d < pairs)
        def _():
            xa_copy(d).start()

    for j in range(2):
        base[j] = jnp.where(k == 1, local[j] + plocal[j], local[j])

    for s in range(1, mid):
        if s > 1:
            pass_on(s, True)
        for way in range(2):
            core_wait(slot(way, s))
            attend(slot(way, s))

    for d in range(1, pairs):
        @pl.when(a >= d)
        def _():
            xa_copy(d).wait_recv()
            ya_copy(d).start()

    ring_copy(0, mid - 1, 0).wait_recv()
    start(core_copy, mid, 0)
    opposite_copy().wait_recv()
    start(core_copy, mid, 1)
    ring_copy(1, mid - 1, CHUNKS - 1).wait_recv()
    start(core_copy, mid, CHUNKS - 1)
    core_wait(mid)

    def last_tile(j, carry):
        keys, values = keys_values(mid, j)
        for g in range(2):
            kbuf[j, g] = keys[g].reshape(2, Rp, HD)
            vbuf[j, g] = values[g].reshape(2, Rp, 2 * HD)
        return carry

    lax.fori_loop(0, tiles, last_tile, 0)
    last_frame = frames_of(mid)

    def finish(b, m, i):
        lo, hi = bands[i]
        allowed = last_frame <= qframe[b, lo:hi]
        for j in range(tiles):
            for g in range(2):
                part = partial_sums(
                    qbuf[j, g, b, lo:hi], kbuf[j, g].reshape(n_rows, HD), vbuf[j, g].reshape(n_rows, 2 * HD), allowed
                )
                full = acc[j, g, b, lo:hi] + part
                first = (2 * j + g) * HD
                atts[m, lo:hi, first:first + HD] = (full[:, :HD] / full[:, HD:]).astype(jnp.bfloat16)

    def away(i):
        return remote(
            band(atts.at[0], i), band(attr.at[k], i), att_send.at[0, i], att_recv.at[k, i],
            {"tm": 2 * a + h, "ctx": (1 - h) * ring + r},
        )

    def across(i):
        return remote(
            band(atts.at[1], i), band(attr.at[k], i), att_send.at[1, i], att_recv.at[k, i], core_peer
        )

    for i in range(2):
        finish(1 - h, 0, i)
        start(away, i)
    for i in range(2):
        finish(h, 1, i)

        @pl.when(k != h)
        def _():
            across(i).start()

    @pl.when(k == h)
    def _():
        attr[k] = atts[1]

    for d in range(1, pairs):
        @pl.when(a >= d)
        def _():
            ya_copy(d).wait_recv()
            base[k] += xar[d - 1]
            base[1 - k] += yar[d - 1]

    loads[4].wait()

    def d_copy(j, i):
        return remote(band(db.at[j], i), band(pdb.at[j], i), d_send.at[j, i], d_recv.at[j, i], core_peer)

    for i in range(2):
        lo, hi = bands[i]
        for m in range(2):
            @pl.when(jnp.logical_not(jnp.logical_and(k == h, k == m)))
            def _():
                remote(
                    band(atts.at[m], i), band(attr.at[m], i), att_send.at[m, i], att_recv.at[m, i],
                    {"tm": 2 * a + m, "ctx": k * ring + r},
                ).wait_recv()

        for j in range(2):
            branch = jnp.zeros((hi - lo, half), jnp.float32)
            for m in range(2):
                branch += jnp.dot(
                    attr[m, lo:hi], wo[m * half:(m + 1) * half, j * half:(j + 1) * half],
                    preferred_element_type=jnp.float32,
                )
            drift[j, lo:hi] = negate[j, lo:hi] * branch
            db[j, lo:hi] = drift[j, lo:hi].astype(jnp.bfloat16)
            start(d_copy, j, i)
        for j in range(2):
            d_copy(j, i).wait_recv()
        xs[lo:hi] = (drift[k, lo:hi] + pdb[k, lo:hi].astype(jnp.float32)).astype(jnp.bfloat16)
        for d in range(1, pairs):
            @pl.when(a + d < pairs)
            def _():
                x_copy(d, i).start()

    for j in range(2):
        here = base[j] + drift[j, :R]
        base[j] = jnp.where(k == 1, here + pdb[j].astype(jnp.float32)[:R], here)

    for d in range(1, pairs):
        @pl.when(a >= d)
        def _():
            for i in range(2):
                x_copy(d, i).wait_recv()
                y_copy(d, i).start()
            base[k] += xr[d - 1].astype(jnp.float32)[:R]
            for i in range(2):
                y_copy(d, i).wait_recv()
            base[1 - k] += yr[d - 1].astype(jnp.float32)[:R]

    for j in range(2):
        out_ref[0, :, j * half:(j + 1) * half] = base[j]

    for make, what in started:
        make(*what).wait_send()

    @pl.when(k != h)
    def _():
        for j in range(CHUNKS):
            swap_copy(j).wait_send()
        for i in range(2):
            across(i).wait_send()

    for d in range(1, pairs):
        @pl.when(a + d < pairs)
        def _():
            xa_copy(d).wait_send()
            for i in range(2):
                x_copy(d, i).wait_send()

        @pl.when(a >= d)
        def _():
            ya_copy(d).wait_send()
            for i in range(2):
                y_copy(d, i).wait_send()


def per_device(tm_size, ctx_size, iterate, anchor, frame_index, noise_steps, qkv_weight, out_weight, mod_weight):
    R, D = anchor.shape
    half = D // 2
    wide = D // CHUNKS
    ring = ctx_size // 2
    pairs = tm_size // 2
    far = max(pairs - 1, 1)
    mid = ring // 2
    Rp = (R + 1 + 15) // 16 * 16
    tiles = half // (2 * HD)
    vmem = pl.BlockSpec(memory_space=pltpu.VMEM)
    hbm = pl.BlockSpec(memory_space=pltpu.HBM)
    dma = pltpu.SemaphoreType.DMA
    f32, bf16 = jnp.float32, jnp.bfloat16
    total = pl.pallas_call(
        functools.partial(kernel, tm_size, ctx_size),
        out_shape=jax.ShapeDtypeStruct((1, R, D), f32),
        in_specs=[vmem, vmem, pl.BlockSpec(memory_space=pltpu.SMEM)] + [hbm] * 3,
        out_specs=vmem,
        scratch_shapes=[
            pltpu.VMEM((3, D, half), bf16),
            pltpu.VMEM((D, D), bf16),
            pltpu.VMEM(mod_weight.shape, bf16),
            pltpu.VMEM((CHUNKS, Rp, wide), bf16),
            pltpu.VMEM((ring, CHUNKS, 2, Rp, wide), bf16),
            pltpu.VMEM((tiles, 2, 2, Rp, HD), bf16),
            pltpu.VMEM((2, Rp, 1), f32),
            pltpu.VMEM((tiles, 2, 2, Rp, 2 * HD), f32),
            pltpu.VMEM((tiles, 2, 2, Rp, HD), bf16),
            pltpu.VMEM((tiles, 2, 2, Rp, 2 * HD), bf16),
            pltpu.VMEM((2, Rp, half), bf16),
            pltpu.VMEM((2, Rp, half), bf16),
            pltpu.VMEM((2, Rp, half), f32),
            pltpu.VMEM((2, R, half), f32),
            pltpu.VMEM((2, R, half), f32),
            pltpu.VMEM((2, R, half), f32),
            pltpu.VMEM((2, Rp, half), f32),
            pltpu.VMEM((2, Rp, half), bf16),
            pltpu.VMEM((2, Rp, half), bf16),
            pltpu.VMEM((R, half), f32),
            pltpu.VMEM((far, R, half), f32),
            pltpu.VMEM((far, R, half), f32),
            pltpu.VMEM((Rp, half), bf16),
            pltpu.VMEM((far, Rp, half), bf16),
            pltpu.VMEM((far, Rp, half), bf16),
            dma((5,)),
            dma((CHUNKS,)), dma((CHUNKS,)),
            dma((2, mid, CHUNKS)), dma((2, mid, CHUNKS)),
            dma, dma,
            dma((ring, CHUNKS)), dma((ring, CHUNKS)),
            dma((2, 2)), dma((2, 2)),
            dma((2,)), dma((2,)),
            dma((2, 2)), dma((2, 2)),
            dma((far,)), dma((far,)),
            dma((far,)), dma((far,)),
            dma((far, 2)), dma((far, 2)),
            dma((far, 2)), dma((far, 2)),
        ],
        compiler_params=pltpu.CompilerParams(
            collective_id=0, has_side_effects=True, vmem_limit_bytes=56 * 1024 * 1024
        ),
    )(iterate, frame_index[None, :], noise_steps, qkv_weight, out_weight, mod_weight)
    return anchor[None] + total


def solution(mesh):
    placed = (P("tm", "ctx", None), P("ctx", None), P("ctx"), P("tm", None), P(), P(), P())
    return jax.shard_map(
        functools.partial(per_device, mesh.shape["tm"], mesh.shape["ctx"]),
        mesh=mesh, in_specs=placed, out_specs=P("tm", "ctx", None), check_vma=False,
    )
```
